512 devices in a mesh: tile: 32 (over y, x, core), aux: 16 (over z).
Axes of the slice: x: 4, y: 4, z: 16, core: 2. Of those that a mesh axis runs over, the one named last changes fastest.
Arguments:
- amplitudes: bfloat16 [128, 128, 128], P('tile'), may hold values from -6 to 6
- df_factors: bfloat16 [1536, 3072], P('aux'), may hold values from -0.15625 to 0.15625
- out_tiles: int32 [1024], P(('tile', 'aux')), may hold values from 0 to 23
- pair_col: int32 [1024, 16], P(('tile', 'aux')), may hold values from 0 to 23
- pair_amp: int32 [1024, 16], replicated, may hold values from 0 to 127, as said below
Outputs:
- residual: bfloat16 [1024, 128, 128], P(('tile', 'aux'))
The draws below stay inside these ranges and needn't reach their ends.
Inputs may be any that keep to these rules, and one draw needn't show every extreme that they name: `pair_amp`: among the 32 entries of the output tiles of one device, no owner occurs more than 2 times, and in every device's entries at least one owner occurs exactly 2 times (several may).
All inputs are finite; a program needn't handle non-finite values.
Results may differ from the reference program's by a relative error of at most 0.0049.
Values may be sent and summed in bfloat16 or wider, within the bound.
A program may use at most 128 MiB of HBM per device.

```python
import jax
import jax.numpy as jnp
from jax import lax

TILE = 128
VT = 24
PAIRS = 16
OD = 2
AMP_DEV = 4
NAUX = 1536
NAMP = 128
NOUT = 1024
NOV = 3072
CAP = 2
N_TILE = 32
N_AUX = 16


def draw_pair_amp(key, part):
    blocks = N_TILE * N_AUX
    per_block = OD * PAIRS
    base_key = jax.random.fold_in(key, 11)
    hot_base = jax.random.randint(jax.random.fold_in(base_key, 1), (), 0, N_TILE)
    hot_owner = (hot_base + jax.random.randint(jax.random.fold_in(base_key, 2), (blocks,), 0, 4)) % N_TILE
    perm_keys = jax.random.split(jax.random.fold_in(base_key, 3), blocks)
    other_slots = jax.vmap(lambda k: jax.random.permutation(k, (N_TILE - 1) * CAP))(perm_keys)
    other_owner = other_slots[:, :per_block - CAP] // CAP
    other_owner = other_owner + (other_owner >= hot_owner[:, None]).astype(jnp.int32)
    owners = jnp.concatenate([jnp.broadcast_to(hot_owner[:, None], (blocks, CAP)), other_owner], axis=1)
    shuffle_keys = jax.random.split(jax.random.fold_in(base_key, 4), blocks)
    orders = jax.vmap(lambda k: jax.random.permutation(k, per_block))(shuffle_keys)
    owners = jnp.take_along_axis(owners, orders, axis=1)
    within = jax.random.randint(jax.random.fold_in(base_key, 5), (blocks, per_block), 0, AMP_DEV)
    amp_ids = owners * AMP_DEV + within
    return amp_ids.reshape(blocks * OD, PAIRS).astype(jnp.int32)


def plant(result, key, low, high):
    dims = result.shape
    spot = [jax.random.randint(jax.random.fold_in(key, axis), (), 0, dims[axis]) for axis in range(len(dims))]
    result = result.at[tuple(spot)].set(low)
    longest = dims.index(max(dims))
    spot[longest] = (spot[longest] + 1) % dims[longest]
    return result.at[tuple(spot)].set(high)


def level_of(key, dims, cuts, least, top_value):
    loudness = 1.0
    for dim, shards_of in cuts:
        heights = jax.random.uniform(jax.random.fold_in(jax.random.fold_in(key, 6), dim), (shards_of,), jnp.float32, least / len(cuts), top_value / len(cuts))
        loudness = loudness * jnp.repeat(jnp.exp(heights), dims[dim] // shards_of).reshape((-1,) + (1,) * (len(dims) - 1 - dim))
    return loudness


def noise(key, dims, scale, limit, pieces=(), held_as=jnp.bfloat16):
    factor_of = level_of(key, dims, pieces, -0.22, 0.18) if pieces else 1.0
    drawn = jax.random.normal(key, dims, jnp.float32) * scale * factor_of
    return jnp.minimum(jnp.maximum(drawn, -limit), limit).astype(held_as)


def setup_inputs(seed: int = 0) -> dict:
    splits = jax.random.split(jax.random.key(seed), 6)
    amplitudes = noise(splits[0], (NAMP, TILE, TILE), 1.0, 6.0, ((0, 32),))
    df_factors = noise(splits[1], (NAUX, NOV), NAUX ** -0.5, 0.15625, ((0, 16),))
    out_tiles = plant(jax.random.randint(splits[2], (NOUT,), 0, VT), jax.random.fold_in(splits[2], 1), 0, VT - 1).astype(jnp.int32)
    pair_col = plant(jax.random.randint(splits[3], (NOUT, PAIRS), 0, VT), jax.random.fold_in(splits[3], 1), 0, VT - 1).astype(jnp.int32)
    pair_amp = draw_pair_amp(jax.random.fold_in(splits[5], 71), 0)
    return {"amplitudes": amplitudes, "df_factors": df_factors, "out_tiles": out_tiles, "pair_col": pair_col, "pair_amp": pair_amp}


def reference(amplitudes, df_factors, out_tiles, pair_col, pair_amp):
    gram_full = jnp.dot(df_factors.T, df_factors, preferred_element_type=jnp.float32)
    panels = gram_full.astype(jnp.bfloat16).reshape(VT, TILE, VT, TILE).transpose(0, 2, 1, 3)

    def one_output(inputs):
        pair_tile, columns, amp_ids = inputs
        blocks = panels[columns, pair_tile].astype(jnp.float32)
        chosen = amplitudes[amp_ids].astype(jnp.float32)
        total = jnp.einsum("kac,kcb->ab", chosen, blocks)
        return total.astype(jnp.bfloat16)

    return lax.map(one_output, (out_tiles, pair_col, pair_amp))
```

```python
import functools

import jax
import jax.numpy as jnp
from jax import lax
from jax.experimental import pallas as pl
from jax.experimental.pallas import tpu as pltpu
from jax.sharding import PartitionSpec as P

MESH = pl.DeviceIdType.MESH
NX = 4
NY = 4
LINE = 4
QUAD = 4
NT = (((1,), (1,)), ((), ()))
NN = (((1,), (0,)), ((), ()))


def kernel(amp_ref, list_ref, a_ref, b_ref, out_ref,
           a_all, b_all, lists_v, lists_s, own, part_s, part_r,
           loc_sem, z_send, z_recv, l_send, l_recv,
           a_send, a_fsend, a_csend, a_recv, a_crecv,
           b_send, b_fsend, b_csend, b_recv, b_crecv,
           r_send, r_recv):
    tile = lax.axis_index("tile")
    z = lax.axis_index("aux")
    core = lax.rem(tile, 2)
    x = lax.rem(tile // 2, NX)
    y = tile // (2 * NX)
    pos = lax.rem(z, LINE)
    base = z - pos
    rows = b_ref.shape[0]
    ctiles = b_all.shape[0]
    nb = ctiles // (2 * NX)
    far = b_all.shape[1] - rows
    half = far // 2

    def at(xx, yy, cc):
        return (yy * NX + xx) * 2 + cc

    def xp(i):
        return lax.rem(x + i, NX)

    def yp(i):
        return lax.rem(y + i, NY)

    def xdev(i):
        return (at(xp(i), y, core), z)

    def ydev(i):
        return (at(x, yp(i), core), z)

    def zdev(i):
        return (tile, lax.rem(z + LINE * i, LINE * QUAD))

    def ldev(i):
        return (tile, base + lax.rem(pos + i, LINE))

    sib = (at(x, y, 1 - core), z)

    def remote(src, dst, ss, rs, dev):
        return pltpu.make_async_remote_copy(
            src_ref=src, dst_ref=dst, send_sem=ss, recv_sem=rs, device_id=dev, device_id_type=MESH)

    def apiece(d, h):
        return a_all.at[pl.ds(d * 4 + 2 * h, 2)]

    def bpiece(d, h):
        return b_all.at[d, pl.ds(rows + half * h, half)]

    own_a = pltpu.make_async_copy(a_ref, a_all.at[pl.ds(tile * 4, 4)], loc_sem.at[0])
    own_a.start()
    b_copies = []
    for c in range(ctiles):
        cp = pltpu.make_async_copy(
            b_ref.at[:, pl.ds(c * 128, 128)], b_all.at[c, pl.ds(0, rows)], loc_sem.at[2 + c])
        cp.start()
        b_copies.append(cp)
    lists_v[pos] = list_ref[...]

    barrier = pltpu.get_barrier_semaphore()
    devs = [f(i) for i in (1, 2, 3) for f in (xdev, ydev, zdev, ldev)] + [sib]
    for dev in devs:
        pl.semaphore_signal(barrier, inc=1, device_id=dev, device_id_type=MESH)
    own_a.wait()
    for cp in b_copies:
        cp.wait()
    pl.semaphore_wait(barrier, len(devs))

    def zcopy(i):
        return remote(b_all.at[tile, pl.ds(0, rows)], b_all.at[tile, pl.ds(rows * (QUAD - i), rows)],
                      z_send.at[i], z_recv.at[QUAD - i], zdev(i))

    def zwait(r):
        return remote(b_all.at[tile, pl.ds(0, rows)], b_all.at[tile, pl.ds(rows * r, rows)],
                      z_send.at[r], z_recv.at[r], zdev(r))

    @pl.when(y < nb)
    def _():
        for i in (2, 1, 3):
            zcopy(i).start()

    def lcopy(i):
        return remote(lists_v.at[pos], lists_v.at[pos], l_send.at[i], l_recv.at[i], ldev(i))

    def lwait(i):
        j = lax.rem(pos + i, LINE)
        return remote(lists_v.at[j], lists_v.at[j], l_send.at[i], l_recv.at[LINE - i], ldev(i))

    def asend(h, k, i, dev):
        return remote(apiece(tile, h), apiece(tile, h), a_send.at[h, k, i], a_recv.at[h, tile // 2], dev)

    for i in (1, 3, 2):
        asend(0, 0, i, xdev(i)).start()
        asend(1, 1, i, ydev(i)).start()
    for i in (1, 3, 2):
        asend(0, 1, i, ydev(i)).start()
        asend(1, 0, i, xdev(i)).start()
    for i in (1, 2, 3):
        lcopy(i).start()

    def whole(d):
        return a_all.at[pl.ds(d * 4, 4)]

    def acore(d):
        return remote(whole(d), whole(d), a_csend.at[d // 2], a_crecv.at[d // 2], sib)

    acore(tile).start()

    def await_a(d, h):
        remote(apiece(d, h), apiece(d, h), a_send.at[0, 0, 0], a_recv.at[h, d // 2], sib).wait_recv()

    def afwd(h, j, i, d, dev):
        return remote(apiece(d, h), apiece(d, h), a_fsend.at[h, j, i], a_recv.at[h, d // 2], dev)

    for j in (1, 3, 2):
        d = at(xp(j), y, core)
        await_a(d, 0)
        for i in (1, 3, 2):
            afwd(0, j, i, d, ydev(i)).start()
        d = at(x, yp(j), core)
        await_a(d, 1)
        for i in (1, 3, 2):
            afwd(1, j, i, d, xdev(i)).start()

    def bsend(h, k, i, dev):
        return remote(bpiece(tile, h), bpiece(tile, h), b_send.at[h, k, i], b_recv.at[h, tile // 2], dev)

    def bwhole(d):
        return b_all.at[d, pl.ds(rows, far)]

    def bcore(d):
        return remote(bwhole(d), bwhole(d), b_csend.at[d // 2], b_crecv.at[d // 2], sib)

    def await_b(d, h):
        remote(bpiece(d, h), bpiece(d, h), b_send.at[0, 0, 0], b_recv.at[h, d // 2], sib).wait_recv()

    def bfwd(h, j, i, d, dev):
        return remote(bpiece(d, h), bpiece(d, h), b_fsend.at[h, j, i], b_recv.at[h, d // 2], dev)

    @pl.when(y < nb)
    def _():
        for r in (1, 2, 3):
            zwait(r).wait_recv()
        for i in (1, 3, 2):
            bsend(0, 0, i, xdev(i)).start()
            bsend(1, 1, i, ydev(i)).start()
        for i in (1, 3, 2):
            bsend(0, 1, i, ydev(i)).start()
            bsend(1, 0, i, xdev(i)).start()
        bcore(tile).start()

    for j in (1, 3, 2):
        @pl.when(y < nb)
        def _():
            d = at(xp(j), y, core)
            await_b(d, 0)
            for i in (1, 3, 2):
                bfwd(0, j, i, d, ydev(i)).start()

        @pl.when(yp(j) < nb)
        def _():
            d = at(x, yp(j), core)
            await_b(d, 1)
            for i in (1, 3, 2):
                bfwd(1, j, i, d, xdev(i)).start()

    def rest_a(d, first, second):
        if first:
            await_a(d, 0)
        if second:
            await_a(d, 1)
        acore(d).start()

    for j in (1, 2, 3):
        rest_a(at(xp(j), y, core), False, True)
        rest_a(at(x, yp(j), core), True, False)
    for i in (1, 2, 3):
        for j in (1, 2, 3):
            rest_a(at(xp(j), yp(i), core), True, True)

    def rest_b(yy, d, first, second):
        @pl.when(yy < nb)
        def _():
            if first:
                await_b(d, 0)
            if second:
                await_b(d, 1)
            bcore(d).start()

    for j in (1, 2, 3):
        rest_b(y, at(xp(j), y, core), False, True)
        rest_b(yp(j), at(x, yp(j), core), True, False)
    for i in (1, 2, 3):
        for j in (1, 2, 3):
            rest_b(yp(i), at(xp(j), yp(i), core), True, True)

    for i in (1, 2, 3):
        lwait(i).wait_recv()
    lists = pltpu.make_async_copy(lists_v, lists_s, loc_sem.at[1])
    lists.start()

    def from_core_a(n, _):
        d = n * 2 + 1 - core
        remote(whole(d), whole(d), a_csend.at[n], a_crecv.at[n], sib).wait_recv()
        return 0

    lax.fori_loop(0, NX * NY, from_core_a, 0)

    def from_core_b(n, _):
        d = n * 2 + 1 - core
        remote(bwhole(d), bwhole(d), b_csend.at[n], b_crecv.at[n], sib).wait_recv()
        return 0

    lax.fori_loop(0, nb * NX, from_core_b, 0)
    lists.wait()

    def partial(p, o):
        total = None
        for k in range(0, 16, 2):
            am = jnp.concatenate([a_all[amp_ref[2 * p + o, k + s]] for s in (0, 1)], axis=1)
            bm = jnp.concatenate([b_all[lists_s[p, o, k + s]] for s in (0, 1)], axis=1)
            term = lax.dot_general(am, bm, NT, preferred_element_type=jnp.float32)
            total = term if total is None else total + term
        right = b_all[lists_s[p, 2 + o, 0]]
        return lax.dot_general(total.astype(jnp.bfloat16), right, NN, preferred_element_type=jnp.float32)

    def rcopy(n, i, o):
        return remote(part_s.at[n], part_r.at[n], r_send.at[n], r_recv.at[n], ldev(i))

    def away(n, _):
        i = n // 2 + 1
        o = lax.rem(n, 2)
        part_s[n] = partial(lax.rem(pos + i, LINE), o).astype(jnp.bfloat16)
        rcopy(n, i, o).start()
        return 0

    lax.fori_loop(0, 6, away, 0)

    def home(o, _):
        own[o] = partial(pos, o)
        return 0

    lax.fori_loop(0, 2, home, 0)

    for n in range(6):
        rcopy(n, n // 2 + 1, n % 2).wait_recv()
    for o in range(2):
        out_ref[o] = (own[o] + part_r[o].astype(jnp.float32) + part_r[2 + o].astype(jnp.float32)
                      + part_r[4 + o].astype(jnp.float32)).astype(jnp.bfloat16)

    for n in range(6):
        rcopy(n, n // 2 + 1, n % 2).wait_send()
    for i in (1, 2, 3):
        lcopy(i).wait_send()
        for h in (0, 1):
            asend(h, 0, i, xdev(i)).wait_send()
            asend(h, 1, i, ydev(i)).wait_send()
            for j in (1, 2, 3):
                if h == 0:
                    afwd(0, j, i, at(xp(j), y, core), ydev(i)).wait_send()
                else:
                    afwd(1, j, i, at(x, yp(j), core), xdev(i)).wait_send()

    def core_sent(n, _):
        acore(n * 2 + core).wait_send()
        return 0

    lax.fori_loop(0, NX * NY, core_sent, 0)

    def bcore_sent(n, _):
        bcore(n * 2 + core).wait_send()
        return 0

    lax.fori_loop(0, nb * NX, bcore_sent, 0)

    @pl.when(y < nb)
    def _():
        for i in (1, 2, 3):
            zcopy(i).wait_send()
            for h in (0, 1):
                bsend(h, 0, i, xdev(i)).wait_send()
                bsend(h, 1, i, ydev(i)).wait_send()
            for j in (1, 2, 3):
                bfwd(0, j, i, at(xp(j), y, core), ydev(i)).wait_send()

    for j in (1, 2, 3):
        @pl.when(yp(j) < nb)
        def _():
            for i in (1, 2, 3):
                bfwd(1, j, i, at(x, yp(j), core), xdev(i)).wait_send()


def body(amplitudes, df_factors, out_tiles, pair_col, pair_amp):
    me_tile = lax.axis_index("tile")
    me_aux = lax.axis_index("aux")
    ts = amplitudes.shape[1]
    rows, cols = df_factors.shape
    ctiles = cols // ts
    start = (me_tile * 16 + (me_aux // LINE) * LINE) * 2
    amps = lax.dynamic_slice_in_dim(pair_amp, start, 2 * LINE, 0)
    lists = jnp.concatenate([pair_col, jnp.broadcast_to(out_tiles[:, None], pair_col.shape)], axis=0)
    lists = jnp.pad(lists, ((0, 4), (0, 128 - pair_col.shape[1])))
    dma = pltpu.SemaphoreType.DMA
    chips = NX * NY
    vmem = pl.BlockSpec(memory_space=pltpu.VMEM)
    anyw = pl.BlockSpec(memory_space=pl.ANY)
    return pl.pallas_call(
        kernel,
        out_shape=jax.ShapeDtypeStruct((2, ts, ts), jnp.bfloat16),
        in_specs=[pl.BlockSpec(memory_space=pltpu.SMEM), vmem, anyw, anyw],
        out_specs=vmem,
        scratch_shapes=[
            pltpu.VMEM((128, ts, ts), jnp.bfloat16),
            pltpu.VMEM((ctiles, QUAD * rows, ts), jnp.bfloat16),
            pltpu.VMEM((LINE, 8, 128), jnp.int32),
            pltpu.SMEM((LINE, 8, 128), jnp.int32),
            pltpu.VMEM((2, ts, ts), jnp.float32),
            pltpu.VMEM((6, ts, ts), jnp.bfloat16),
            pltpu.VMEM((6, ts, ts), jnp.bfloat16),
            dma((2 + ctiles,)), dma((4,)), dma((4,)), dma((4,)), dma((4,)),
            dma((2, 2, 4)), dma((2, 4, 4)), dma((chips,)), dma((2, chips)), dma((chips,)),
            dma((2, 2, 4)), dma((2, 4, 4)), dma((chips,)), dma((2, chips)), dma((chips,)),
            dma((6,)), dma((6,)),
        ],
        compiler_params=pltpu.CompilerParams(
            collective_id=0, has_side_effects=True, vmem_limit_bytes=40 * 2**20),
        name="residual",
    )(amps, lists, amplitudes, df_factors)


def solution(mesh):
    in_specs = (
        P("tile", None, None),
        P("aux", None),
        P(("tile", "aux")),
        P(("tile", "aux"), None),
        P(),
    )
    out_specs = P(("tile", "aux"), None, None)
    return jax.shard_map(body, mesh=mesh, in_specs=in_specs, out_specs=out_specs, check_vma=False)
```

```python
import functools

import jax
import jax.numpy as jnp
from jax import lax
from jax.experimental import pallas as pl
from jax.experimental.pallas import tpu as pltpu
from jax.sharding import PartitionSpec as P

MESH = pl.DeviceIdType.MESH
NX = 4
NY = 4
LINE = 4
QUAD = 4
NT = (((1,), (1,)), ((), ()))
NN = (((1,), (0,)), ((), ()))


def kernel(amp_ref, col_ref, tgt_ref, a_ref, b_ref, out_ref,
           a_all, b_all, cols_v, tgts_v, amp_s, cols_s, tgts_s, own, part_s, part_r,
           loc_sem, z_ack, l_ack, z_send, z_recv, l_send, l_recv,
           a_send, a_fsend, a_csend, a_recv, a_crecv,
           b_send, b_fsend, b_csend, b_recv, b_crecv,
           r_send, r_recv):
    tile = lax.axis_index("tile")
    z = lax.axis_index("aux")
    core = lax.rem(tile, 2)
    x = lax.rem(tile // 2, NX)
    y = tile // (2 * NX)
    pos = lax.rem(z, LINE)
    rank = z // LINE
    base = z - pos
    rows = b_ref.shape[0]
    ctiles = b_all.shape[0]
    nb = ctiles // (2 * NX)
    first = (rows, 2 * rows)
    count = (rows, 2 * rows)

    def at(xx, yy, cc):
        return (yy * NX + xx) * 2 + cc

    def xp(i):
        return lax.rem(x + i, NX)

    def yp(i):
        return lax.rem(y + i, NY)

    def xdev(i):
        return (at(xp(i), y, core), z)

    def ydev(i):
        return (at(x, yp(i), core), z)

    def zdev(i):
        return (tile, lax.rem(z + LINE * i, LINE * QUAD))

    def ldev(i):
        return (tile, base + lax.rem(pos + i, LINE))

    sib = (at(x, y, 1 - core), z)
    mine = (tile * LINE * QUAD + base) * 2

    def remote(src, dst, ss, rs, dev):
        return pltpu.make_async_remote_copy(
            src_ref=src, dst_ref=dst, send_sem=ss, recv_sem=rs, device_id=dev, device_id_type=MESH)

    def signal(sem, dev):
        pl.semaphore_signal(sem, inc=1, device_id=dev, device_id_type=MESH)

    local = [
        pltpu.make_async_copy(a_ref, a_all.at[pl.ds(tile * 4, 4)], loc_sem.at[0]),
        pltpu.make_async_copy(col_ref, cols_v.at[pos], loc_sem.at[1]),
        pltpu.make_async_copy(tgt_ref, tgts_v.at[pos], loc_sem.at[2]),
        pltpu.make_async_copy(
            amp_ref.at[:, pl.ds(pl.multiple_of(mine - lax.rem(mine, 128), 128), 128)], amp_s, loc_sem.at[3]),
    ]
    for c in range(ctiles):
        local.append(pltpu.make_async_copy(
            b_ref.at[:, pl.ds(c * 128, 128)], b_all.at[c, pl.ds(0, rows)], loc_sem.at[6 + c]))

    barrier = pltpu.get_barrier_semaphore()
    near = [f(i) for i in (1, 2, 3) for f in (xdev, ydev)] + [sib]
    for dev in near:
        signal(barrier, dev)
    for i in (1, 2, 3):
        @pl.when(rank + i < QUAD)
        def _():
            signal(barrier, zdev(i))

        @pl.when(pos + i < LINE)
        def _():
            signal(barrier, ldev(i))
    for cp in local:
        cp.start()
    for cp in local:
        cp.wait()
    pl.semaphore_wait(barrier, len(near) + rank + pos)
    for i in (1, 2, 3):
        @pl.when(rank + i >= QUAD)
        def _():
            signal(z_ack.at[QUAD - i], zdev(i))

        @pl.when(pos + i >= LINE)
        def _():
            signal(l_ack.at[LINE - i], ldev(i))

    def zcopy(i):
        return remote(b_all.at[tile, pl.ds(0, rows)], b_all.at[tile, pl.ds(rows * (QUAD - i), rows)],
                      z_send.at[i], z_recv.at[QUAD - i], zdev(i))

    def zwait(r):
        remote(b_all.at[tile, pl.ds(0, rows)], b_all.at[tile, pl.ds(rows * r, rows)],
               z_send.at[r], z_recv.at[r], zdev(r)).wait_recv()

    def zup(i, ranks):
        for r in ranks:
            @pl.when(rank == r)
            def _():
                pl.semaphore_wait(z_ack.at[i], 1)

                @pl.when(y < nb)
                def _():
                    zcopy(i).start()

    for i in (2, 1, 3):
        @pl.when((rank + i >= QUAD) & (y < nb))
        def _():
            zcopy(i).start()

    def lcopies(i):
        return [remote(v.at[pos], v.at[pos], l_send.at[n, i], l_recv.at[n, i], ldev(i))
                for n, v in enumerate((cols_v, tgts_v))]

    def lwaits(i):
        j = lax.rem(pos + i, LINE)
        for n, v in enumerate((cols_v, tgts_v)):
            remote(v.at[j], v.at[j], l_send.at[n, i], l_recv.at[n, LINE - i], ldev(i)).wait_recv()

    def apiece(d, h):
        return a_all.at[pl.ds(d * 4 + 2 * h, 2)]

    def whole(d):
        return a_all.at[pl.ds(d * 4, 4)]

    def asend(h, k, i, dev):
        return remote(apiece(tile, h), apiece(tile, h), a_send.at[h, k, i], a_recv.at[h, tile // 2], dev)

    def acore(d):
        return remote(whole(d), whole(d), a_csend.at[d // 2], a_crecv.at[d // 2], sib)

    def await_a(d, h):
        remote(apiece(d, h), apiece(d, h), a_send.at[0, 0, 0], a_recv.at[h, d // 2], sib).wait_recv()

    def afwd(h, j, i, d, dev):
        return remote(apiece(d, h), apiece(d, h), a_fsend.at[h, j, i], a_recv.at[h, d // 2], dev)

    for i in (1, 3, 2):
        asend(0, 0, i, xdev(i)).start()
        asend(1, 1, i, ydev(i)).start()
    for i in (1, 3, 2):
        asend(0, 1, i, ydev(i)).start()
        asend(1, 0, i, xdev(i)).start()
    for i in (1, 2, 3):
        @pl.when(pos + i >= LINE)
        def _():
            for cp in lcopies(i):
                cp.start()
    acore(tile).start()

    for j in (1, 3, 2):
        d = at(xp(j), y, core)
        await_a(d, 0)
        for i in (1, 3, 2):
            afwd(0, j, i, d, ydev(i)).start()
        d = at(x, yp(j), core)
        await_a(d, 1)
        for i in (1, 3, 2):
            afwd(1, j, i, d, xdev(i)).start()

    zup(1, (0, 1, 2))
    zup(2, (1,))
    for i in (1, 2, 3):
        @pl.when(pos + i < LINE)
        def _():
            pl.semaphore_wait(l_ack.at[i], 1)
            for cp in lcopies(i):
                cp.start()

    def bpiece(s, d, h):
        return b_all.at[d, pl.ds(first[s] + count[s] // 2 * h, count[s] // 2)]

    def bwhole(s, d):
        return b_all.at[d, pl.ds(first[s], count[s])]

    def bsend(s, h, k, i, dev):
        return remote(bpiece(s, tile, h), bpiece(s, tile, h), b_send.at[s, h, k, i], b_recv.at[s, h, tile // 2], dev)

    def bcore(s, d):
        return remote(bwhole(s, d), bwhole(s, d), b_csend.at[s, d // 2], b_crecv.at[s, d // 2], sib)

    def await_b(s, d, h):
        remote(bpiece(s, d, h), bpiece(s, d, h), b_send.at[s, 0, 0, 0], b_recv.at[s, h, d // 2], sib).wait_recv()

    def bfwd(s, h, j, i, d, dev):
        return remote(bpiece(s, d, h), bpiece(s, d, h), b_fsend.at[s, h, j, i], b_recv.at[s, h, d // 2], dev)

    def b_own(s):
        @pl.when(y < nb)
        def _():
            for r in ((1,), (2, 3))[s]:
                zwait(r)
            for i in (1, 3, 2):
                bsend(s, 0, 0, i, xdev(i)).start()
                bsend(s, 1, 1, i, ydev(i)).start()
            for i in (1, 3, 2):
                bsend(s, 0, 1, i, ydev(i)).start()
                bsend(s, 1, 0, i, xdev(i)).start()
            bcore(s, tile).start()

    def b_forward(s):
        for j in (1, 3, 2):
            @pl.when(y < nb)
            def _():
                d = at(xp(j), y, core)
                await_b(s, d, 0)
                for i in (1, 3, 2):
                    bfwd(s, 0, j, i, d, ydev(i)).start()

            @pl.when(yp(j) < nb)
            def _():
                d = at(x, yp(j), core)
                await_b(s, d, 1)
                for i in (1, 3, 2):
                    bfwd(s, 1, j, i, d, xdev(i)).start()

    def rest_b(s, yy, d, zero, one):
        @pl.when(yy < nb)
        def _():
            if zero:
                await_b(s, d, 0)
            if one:
                await_b(s, d, 1)
            bcore(s, d).start()

    def b_rest(s):
        for j in (1, 2, 3):
            rest_b(s, y, at(xp(j), y, core), False, True)
            rest_b(s, yp(j), at(x, yp(j), core), True, False)
        for i in (1, 2, 3):
            for j in (1, 2, 3):
                rest_b(s, yp(i), at(xp(j), yp(i), core), True, True)

    def rest_a(d, zero, one):
        if zero:
            await_a(d, 0)
        if one:
            await_a(d, 1)
        acore(d).start()

    b_own(0)
    for j in (1, 2, 3):
        rest_a(at(xp(j), y, core), False, True)
        rest_a(at(x, yp(j), core), True, False)
    for i in (1, 2, 3):
        for j in (1, 2, 3):
            rest_a(at(xp(j), yp(i), core), True, True)
    b_forward(0)
    zup(2, (0,))
    zup(3, (0,))
    b_own(1)
    b_rest(0)
    for i in (1, 2, 3):
        lwaits(i)
    lists = [pltpu.make_async_copy(cols_v, cols_s, loc_sem.at[4]),
             pltpu.make_async_copy(tgts_v, tgts_s, loc_sem.at[5])]
    for cp in lists:
        cp.start()
    b_forward(1)
    b_rest(1)

    def from_core_a(n, _):
        d = n * 2 + 1 - core
        remote(whole(d), whole(d), a_csend.at[n], a_crecv.at[n], sib).wait_recv()
        return 0

    lax.fori_loop(0, NX * NY, from_core_a, 0)

    def from_core_b(n, _):
        d = n * 2 + 1 - core
        for s in (0, 1):
            remote(bwhole(s, d), bwhole(s, d), b_csend.at[s, n], b_crecv.at[s, n], sib).wait_recv()
        return 0

    lax.fori_loop(0, nb * NX, from_core_b, 0)
    for cp in lists:
        cp.wait()

    def left(p, o):
        total = None
        for k in range(0, 16, 2):
            am = jnp.concatenate([a_all[amp_s[k + s, lax.rem(mine, 128) + 2 * p + o]] for s in (0, 1)], axis=1)
            bm = jnp.concatenate([b_all[cols_s[p, o, k + s]] for s in (0, 1)], axis=1)
            term = lax.dot_general(am, bm, NT, preferred_element_type=jnp.float32)
            total = term if total is None else total + term
        return total.astype(jnp.bfloat16)

    def partial(p):
        both = [left(p, o) for o in (0, 1)]
        return [lax.dot_general(both[o], b_all[tgts_s[p, 0, o]], NN, preferred_element_type=jnp.float32) for o in (0, 1)]

    def rcopy(i, o):
        n = (i - 1) * 2 + o
        return remote(part_s.at[n], part_r.at[n], r_send.at[n], r_recv.at[n], ldev(i))

    def away(n, _):
        i = n + 1
        for o, r in enumerate(partial(lax.rem(pos + i, LINE))):
            part_s[2 * n + o] = r.astype(jnp.bfloat16)
            rcopy(i, o).start()
        return 0

    lax.fori_loop(0, LINE - 1, away, 0)
    for o, r in enumerate(partial(pos)):
        own[o] = r

    for i in (1, 2, 3):
        for o in (0, 1):
            rcopy(i, o).wait_recv()
    for o in range(2):
        out_ref[o] = (own[o] + part_r[o].astype(jnp.float32) + part_r[2 + o].astype(jnp.float32)
                      + part_r[4 + o].astype(jnp.float32)).astype(jnp.bfloat16)

    for i in (1, 2, 3):
        for o in (0, 1):
            rcopy(i, o).wait_send()
        for cp in lcopies(i):
            cp.wait_send()
        for h in (0, 1):
            asend(h, 0, i, xdev(i)).wait_send()
            asend(h, 1, i, ydev(i)).wait_send()
        for j in (1, 2, 3):
            afwd(0, j, i, at(xp(j), y, core), ydev(i)).wait_send()
            afwd(1, j, i, at(x, yp(j), core), xdev(i)).wait_send()

    def core_sent(n, _):
        acore(n * 2 + core).wait_send()
        return 0

    lax.fori_loop(0, NX * NY, core_sent, 0)

    def bcore_sent(n, _):
        for s in (0, 1):
            bcore(s, n * 2 + core).wait_send()
        return 0

    lax.fori_loop(0, nb * NX, bcore_sent, 0)

    @pl.when(y < nb)
    def _():
        for i in (1, 2, 3):
            zcopy(i).wait_send()
            for s in (0, 1):
                for h in (0, 1):
                    bsend(s, h, 0, i, xdev(i)).wait_send()
                    bsend(s, h, 1, i, ydev(i)).wait_send()
                for j in (1, 2, 3):
                    bfwd(s, 0, j, i, at(xp(j), y, core), ydev(i)).wait_send()

    for j in (1, 2, 3):
        @pl.when(yp(j) < nb)
        def _():
            for i in (1, 2, 3):
                for s in (0, 1):
                    bfwd(s, 1, j, i, at(x, yp(j), core), xdev(i)).wait_send()


def body(amplitudes, df_factors, out_tiles, pair_col, pair_amp):
    ts = amplitudes.shape[1]
    rows, cols = df_factors.shape
    ctiles = cols // ts
    pairs = pair_col.shape[1]
    dma = pltpu.SemaphoreType.DMA
    reg = pltpu.SemaphoreType.REGULAR
    chips = NX * NY
    anyw = pl.BlockSpec(memory_space=pl.ANY)
    return pl.pallas_call(
        kernel,
        out_shape=jax.ShapeDtypeStruct((2, ts, ts), jnp.bfloat16),
        in_specs=[anyw] * 5,
        out_specs=pl.BlockSpec(memory_space=pltpu.VMEM),
        scratch_shapes=[
            pltpu.VMEM((4 * 2 * chips, ts, ts), jnp.bfloat16),
            pltpu.VMEM((ctiles, QUAD * rows, ts), jnp.bfloat16),
            pltpu.VMEM((LINE, 2, pairs), jnp.int32),
            pltpu.VMEM((LINE, 1, 2), jnp.int32),
            pltpu.SMEM((pairs, 128), jnp.int32),
            pltpu.SMEM((LINE, 2, pairs), jnp.int32),
            pltpu.SMEM((LINE, 1, 2), jnp.int32),
            pltpu.VMEM((2, ts, ts), jnp.float32),
            pltpu.VMEM((6, ts, ts), jnp.bfloat16),
            pltpu.VMEM((6, ts, ts), jnp.bfloat16),
            dma((6 + ctiles,)), reg((4,)), reg((4,)), dma((4,)), dma((4,)), dma((2, 4)), dma((2, 4)),
            dma((2, 2, 4)), dma((2, 4, 4)), dma((chips,)), dma((2, chips)), dma((chips,)),
            dma((2, 2, 2, 4)), dma((2, 2, 4, 4)), dma((2, chips)), dma((2, 2, chips)), dma((2, chips)),
            dma((6,)), dma((6,)),
        ],
        compiler_params=pltpu.CompilerParams(
            collective_id=0, has_side_effects=True, vmem_limit_bytes=56 * 2**20),
        name="residual",
    )(pair_amp.T, pair_col, out_tiles[None], amplitudes, df_factors)


def solution(mesh):
    in_specs = (
        P("tile", None, None),
        P("aux", None),
        P(("tile", "aux")),
        P(("tile", "aux"), None),
        P(),
    )
    out_specs = P(("tile", "aux"), None, None)
    return jax.shard_map(body, mesh=mesh, in_specs=in_specs, out_specs=out_specs, check_vma=False)
```

```python
import functools

import jax
import jax.numpy as jnp
from jax import lax
from jax.experimental import pallas as pl
from jax.experimental.pallas import tpu as pltpu
from jax.sharding import PartitionSpec as P

MESH = pl.DeviceIdType.MESH
NX = 4
NY = 4
LINE = 4
QUAD = 4
NT = (((1,), (1,)), ((), ()))
NN = (((1,), (0,)), ((), ()))


def kernel(amp_ref, col_ref, tgt_ref, a_ref, b_ref, out_ref,
           a_all, b_all, cols_v, tgts_v, amp_s, cols_s, tgts_s, own, part_s, part_r,
           loc_sem, z_ack, l_ack, z_send, z_recv, l_send, l_recv,
           a_send, a_fsend, a_csend, a_recv, a_crecv,
           b_send, b_fsend, b_csend, b_recv, b_crecv,
           r_send, r_recv):
    tile = lax.axis_index("tile")
    z = lax.axis_index("aux")
    core = lax.rem(tile, 2)
    x = lax.rem(tile // 2, NX)
    y = tile // (2 * NX)
    pos = lax.rem(z, LINE)
    rank = z // LINE
    base = z - pos
    rows = b_ref.shape[0]
    ctiles = b_all.shape[0]
    nb = ctiles // (2 * NX)
    first = (rows, 3 * rows)
    count = (2 * rows, rows)
    slot = (0, 1, 3, 2)

    def at(xx, yy, cc):
        return (yy * NX + xx) * 2 + cc

    def xp(i):
        return lax.rem(x + i, NX)

    def yp(i):
        return lax.rem(y + i, NY)

    def xdev(i):
        return (at(xp(i), y, core), z)

    def ydev(i):
        return (at(x, yp(i), core), z)

    def zdev(i):
        return (tile, lax.rem(z + LINE * i, LINE * QUAD))

    def ldev(i):
        return (tile, base + lax.rem(pos + i, LINE))

    sib = (at(x, y, 1 - core), z)
    mine = (tile * LINE * QUAD + base) * 2

    def remote(src, dst, ss, rs, dev):
        return pltpu.make_async_remote_copy(
            src_ref=src, dst_ref=dst, send_sem=ss, recv_sem=rs, device_id=dev, device_id_type=MESH)

    def signal(sem, dev):
        pl.semaphore_signal(sem, inc=1, device_id=dev, device_id_type=MESH)

    local = [
        pltpu.make_async_copy(a_ref, a_all.at[pl.ds(tile * 4, 4)], loc_sem.at[0]),
        pltpu.make_async_copy(col_ref, cols_v.at[pos], loc_sem.at[1]),
        pltpu.make_async_copy(tgt_ref, tgts_v.at[pos], loc_sem.at[2]),
        pltpu.make_async_copy(
            amp_ref.at[:, pl.ds(pl.multiple_of(mine - lax.rem(mine, 128), 128), 128)], amp_s, loc_sem.at[3]),
    ]
    for c in range(ctiles):
        local.append(pltpu.make_async_copy(
            b_ref.at[:, pl.ds(c * 128, 128)], b_all.at[c, pl.ds(0, rows)], loc_sem.at[6 + c]))

    barrier = pltpu.get_barrier_semaphore()
    near = [f(i) for i in (1, 2, 3) for f in (xdev, ydev)] + [sib]
    for dev in near:
        signal(barrier, dev)
    for i in (1, 2, 3):
        @pl.when(rank + i < QUAD)
        def _():
            signal(barrier, zdev(i))

        @pl.when(pos + i < LINE)
        def _():
            signal(barrier, ldev(i))
    for cp in local:
        cp.start()
    for cp in local:
        cp.wait()
    pl.semaphore_wait(barrier, len(near) + rank + pos)
    for i in (1, 2, 3):
        @pl.when(rank + i >= QUAD)
        def _():
            signal(z_ack.at[QUAD - i], zdev(i))

        @pl.when(pos + i >= LINE)
        def _():
            signal(l_ack.at[LINE - i], ldev(i))

    def zcopy(i):
        return remote(b_all.at[tile, pl.ds(0, rows)], b_all.at[tile, pl.ds(rows * slot[QUAD - i], rows)],
                      z_send.at[i], z_recv.at[QUAD - i], zdev(i))

    def zwait(r):
        remote(b_all.at[tile, pl.ds(0, rows)], b_all.at[tile, pl.ds(rows * slot[r], rows)],
               z_send.at[r], z_recv.at[r], zdev(r)).wait_recv()

    def zup(i, ranks):
        for r in ranks:
            @pl.when(rank == r)
            def _():
                pl.semaphore_wait(z_ack.at[i], 1)

                @pl.when(y < nb)
                def _():
                    zcopy(i).start()

    for i in (2, 1, 3):
        @pl.when((rank + i >= QUAD) & (y < nb))
        def _():
            zcopy(i).start()

    def lcopies(i):
        return [remote(v.at[pos], v.at[pos], l_send.at[n, i], l_recv.at[n, i], ldev(i))
                for n, v in enumerate((cols_v, tgts_v))]

    def lwaits(i):
        j = lax.rem(pos + i, LINE)
        for n, v in enumerate((cols_v, tgts_v)):
            remote(v.at[j], v.at[j], l_send.at[n, i], l_recv.at[n, LINE - i], ldev(i)).wait_recv()

    def apiece(d, h):
        return a_all.at[pl.ds(d * 4 + 2 * h, 2)]

    def whole(d):
        return a_all.at[pl.ds(d * 4, 4)]

    def asend(h, k, i, dev):
        return remote(apiece(tile, h), apiece(tile, h), a_send.at[h, k, i], a_recv.at[h, tile // 2], dev)

    def acore(d):
        return remote(whole(d), whole(d), a_csend.at[d // 2], a_crecv.at[d // 2], sib)

    def await_a(d, h):
        remote(apiece(d, h), apiece(d, h), a_send.at[0, 0, 0], a_recv.at[h, d // 2], sib).wait_recv()

    def afwd(h, j, i, d, dev):
        return remote(apiece(d, h), apiece(d, h), a_fsend.at[h, j, i], a_recv.at[h, d // 2], dev)

    for i in (1, 3, 2):
        asend(0, 0, i, xdev(i)).start()
        asend(1, 1, i, ydev(i)).start()
    for i in (1, 3, 2):
        asend(0, 1, i, ydev(i)).start()
        asend(1, 0, i, xdev(i)).start()
    for i in (1, 2, 3):
        @pl.when(pos + i >= LINE)
        def _():
            for cp in lcopies(i):
                cp.start()
    acore(tile).start()

    for j in (1, 3, 2):
        d = at(xp(j), y, core)
        await_a(d, 0)
        for i in (1, 3, 2):
            afwd(0, j, i, d, ydev(i)).start()
        d = at(x, yp(j), core)
        await_a(d, 1)
        for i in (1, 3, 2):
            afwd(1, j, i, d, xdev(i)).start()
        if j == 1:
            zup(1, (2,))

    zup(1, (0, 1))
    zup(2, (1,))
    for i in (1, 2, 3):
        @pl.when(pos + i < LINE)
        def _():
            pl.semaphore_wait(l_ack.at[i], 1)
            for cp in lcopies(i):
                cp.start()

    def bpiece(s, d, h):
        return b_all.at[d, pl.ds(first[s] + count[s] // 2 * h, count[s] // 2)]

    def bwhole(s, d):
        return b_all.at[d, pl.ds(first[s], count[s])]

    def bsend(s, h, k, i, dev):
        return remote(bpiece(s, tile, h), bpiece(s, tile, h), b_send.at[s, h, k, i], b_recv.at[s, h, tile // 2], dev)

    def bcore(s, d):
        return remote(bwhole(s, d), bwhole(s, d), b_csend.at[s, d // 2], b_crecv.at[s, d // 2], sib)

    def await_b(s, d, h):
        remote(bpiece(s, d, h), bpiece(s, d, h), b_send.at[s, 0, 0, 0], b_recv.at[s, h, d // 2], sib).wait_recv()

    def bfwd(s, h, j, i, d, dev):
        return remote(bpiece(s, d, h), bpiece(s, d, h), b_fsend.at[s, h, j, i], b_recv.at[s, h, d // 2], dev)

    def b_own(s):
        @pl.when(y < nb)
        def _():
            for r in ((1, 3), (2,))[s]:
                zwait(r)
            for i in (1, 3, 2):
                bsend(s, 0, 0, i, xdev(i)).start()
                bsend(s, 1, 1, i, ydev(i)).start()
            for i in (1, 3, 2):
                bsend(s, 0, 1, i, ydev(i)).start()
                bsend(s, 1, 0, i, xdev(i)).start()
            bcore(s, tile).start()

    def b_forward(s):
        for j in (1, 3, 2):
            @pl.when(y < nb)
            def _():
                d = at(xp(j), y, core)
                await_b(s, d, 0)
                for i in (1, 3, 2):
                    bfwd(s, 0, j, i, d, ydev(i)).start()

            @pl.when(yp(j) < nb)
            def _():
                d = at(x, yp(j), core)
                await_b(s, d, 1)
                for i in (1, 3, 2):
                    bfwd(s, 1, j, i, d, xdev(i)).start()

    def rest_b(s, yy, d, zero, one):
        @pl.when(yy < nb)
        def _():
            if zero:
                await_b(s, d, 0)
            if one:
                await_b(s, d, 1)
            bcore(s, d).start()

    def b_rest(s):
        for j in (1, 2, 3):
            rest_b(s, y, at(xp(j), y, core), False, True)
            rest_b(s, yp(j), at(x, yp(j), core), True, False)
        for i in (1, 2, 3):
            for j in (1, 2, 3):
                rest_b(s, yp(i), at(xp(j), yp(i), core), True, True)

    def rest_a(d, zero, one):
        if zero:
            await_a(d, 0)
        if one:
            await_a(d, 1)
        acore(d).start()

    for j in (1, 2, 3):
        rest_a(at(xp(j), y, core), False, True)
        rest_a(at(x, yp(j), core), True, False)
    zup(3, (0,))
    b_own(0)
    for i in (1, 3, 2):
        for j in (1, 3, 2):
            rest_a(at(xp(j), yp(i), core), True, True)
        if i == 1:
            zup(2, (0,))
        if i == 3:
            b_forward(0)
            b_own(1)
    b_forward(1)
    b_rest(0)
    for i in (1, 2, 3):
        lwaits(i)
    lists = [pltpu.make_async_copy(cols_v, cols_s, loc_sem.at[4]),
             pltpu.make_async_copy(tgts_v, tgts_s, loc_sem.at[5])]
    for cp in lists:
        cp.start()
    b_rest(1)

    def from_core_a(n, _):
        d = n * 2 + 1 - core
        remote(whole(d), whole(d), a_csend.at[n], a_crecv.at[n], sib).wait_recv()
        return 0

    lax.fori_loop(0, NX * NY, from_core_a, 0)

    def from_core_b(n, _):
        d = n * 2 + 1 - core
        for s in (0, 1):
            remote(bwhole(s, d), bwhole(s, d), b_csend.at[s, n], b_crecv.at[s, n], sib).wait_recv()
        return 0

    lax.fori_loop(0, nb * NX, from_core_b, 0)
    for cp in lists:
        cp.wait()

    def left(p, o):
        total = None
        for k in range(0, 16, 2):
            am = jnp.concatenate([a_all[amp_s[k + s, lax.rem(mine, 128) + 2 * p + o]] for s in (0, 1)], axis=1)
            bm = jnp.concatenate([b_all[cols_s[p, o, k + s]] for s in (0, 1)], axis=1)
            term = lax.dot_general(am, bm, NT, preferred_element_type=jnp.float32)
            total = term if total is None else total + term
        return total.astype(jnp.bfloat16)

    def partial(p):
        both = [left(p, o) for o in (0, 1)]
        return [lax.dot_general(both[o], b_all[tgts_s[p, 0, o]], NN, preferred_element_type=jnp.float32) for o in (0, 1)]

    def rcopy(i, o):
        n = (i - 1) * 2 + o
        return remote(part_s.at[n], part_r.at[n], r_send.at[n], r_recv.at[n], ldev(i))

    def away(n, _):
        i = n + 1
        for o, r in enumerate(partial(lax.rem(pos + i, LINE))):
            part_s[2 * n + o] = r.astype(jnp.bfloat16)
            rcopy(i, o).start()
        return 0

    lax.fori_loop(0, LINE - 1, away, 0)
    for o, r in enumerate(partial(pos)):
        own[o] = r

    for i in (1, 2, 3):
        for o in (0, 1):
            rcopy(i, o).wait_recv()
    for o in range(2):
        out_ref[o] = (own[o] + part_r[o].astype(jnp.float32) + part_r[2 + o].astype(jnp.float32)
                      + part_r[4 + o].astype(jnp.float32)).astype(jnp.bfloat16)

    for i in (1, 2, 3):
        for o in (0, 1):
            rcopy(i, o).wait_send()
        for cp in lcopies(i):
            cp.wait_send()
        for h in (0, 1):
            asend(h, 0, i, xdev(i)).wait_send()
            asend(h, 1, i, ydev(i)).wait_send()
        for j in (1, 2, 3):
            afwd(0, j, i, at(xp(j), y, core), ydev(i)).wait_send()
            afwd(1, j, i, at(x, yp(j), core), xdev(i)).wait_send()

    def core_sent(n, _):
        acore(n * 2 + core).wait_send()
        return 0

    lax.fori_loop(0, NX * NY, core_sent, 0)

    def bcore_sent(n, _):
        for s in (0, 1):
            bcore(s, n * 2 + core).wait_send()
        return 0

    lax.fori_loop(0, nb * NX, bcore_sent, 0)

    @pl.when(y < nb)
    def _():
        for i in (1, 2, 3):
            zcopy(i).wait_send()
            for s in (0, 1):
                for h in (0, 1):
                    bsend(s, h, 0, i, xdev(i)).wait_send()
                    bsend(s, h, 1, i, ydev(i)).wait_send()
                for j in (1, 2, 3):
                    bfwd(s, 0, j, i, at(xp(j), y, core), ydev(i)).wait_send()

    for j in (1, 2, 3):
        @pl.when(yp(j) < nb)
        def _():
            for i in (1, 2, 3):
                for s in (0, 1):
                    bfwd(s, 1, j, i, at(x, yp(j), core), xdev(i)).wait_send()


def body(amplitudes, df_factors, out_tiles, pair_col, pair_amp):
    ts = amplitudes.shape[1]
    rows, cols = df_factors.shape
    ctiles = cols // ts
    pairs = pair_col.shape[1]
    dma = pltpu.SemaphoreType.DMA
    reg = pltpu.SemaphoreType.REGULAR
    chips = NX * NY
    anyw = pl.BlockSpec(memory_space=pl.ANY)
    return pl.pallas_call(
        kernel,
        out_shape=jax.ShapeDtypeStruct((2, ts, ts), jnp.bfloat16),
        in_specs=[anyw] * 5,
        out_specs=pl.BlockSpec(memory_space=pltpu.VMEM),
        scratch_shapes=[
            pltpu.VMEM((4 * 2 * chips, ts, ts), jnp.bfloat16),
            pltpu.VMEM((ctiles, QUAD * rows, ts), jnp.bfloat16),
            pltpu.VMEM((LINE, 2, pairs), jnp.int32),
            pltpu.VMEM((LINE, 1, 2), jnp.int32),
            pltpu.SMEM((pairs, 128), jnp.int32),
            pltpu.SMEM((LINE, 2, pairs), jnp.int32),
            pltpu.SMEM((LINE, 1, 2), jnp.int32),
            pltpu.VMEM((2, ts, ts), jnp.float32),
            pltpu.VMEM((6, ts, ts), jnp.bfloat16),
            pltpu.VMEM((6, ts, ts), jnp.bfloat16),
            dma((6 + ctiles,)), reg((4,)), reg((4,)), dma((4,)), dma((4,)), dma((2, 4)), dma((2, 4)),
            dma((2, 2, 4)), dma((2, 4, 4)), dma((chips,)), dma((2, chips)), dma((chips,)),
            dma((2, 2, 2, 4)), dma((2, 2, 4, 4)), dma((2, chips)), dma((2, 2, chips)), dma((2, chips)),
            dma((6,)), dma((6,)),
        ],
        compiler_params=pltpu.CompilerParams(
            collective_id=0, has_side_effects=True, vmem_limit_bytes=56 * 2**20),
        name="residual",
    )(pair_amp.T, pair_col, out_tiles[None], amplitudes, df_factors)


def solution(mesh):
    in_specs = (
        P("tile", None, None),
        P("aux", None),
        P(("tile", "aux")),
        P(("tile", "aux"), None),
        P(),
    )
    out_specs = P(("tile", "aux"), None, None)
    return jax.shard_map(body, mesh=mesh, in_specs=in_specs, out_specs=out_specs, check_vma=False)
```

```python
import functools

import jax
import jax.numpy as jnp
from jax import lax
from jax.experimental import pallas as pl
from jax.experimental.pallas import tpu as pltpu
from jax.sharding import PartitionSpec as P

MESH = pl.DeviceIdType.MESH
NX = 4
NY = 4
LINE = 4
QUAD = 4
NT = (((1,), (1,)), ((), ()))
NN = (((1,), (0,)), ((), ()))


def kernel(amp_ref, col_ref, tgt_ref, a_ref, b_ref, out_ref,
           a_all, b_all, cols_v, tgts_v, amp_s, cols_s, tgts_s, own, part_s, part_r,
           loc_sem, p_ack, z_ack, l_ack, z_send, z_recv, l_send, l_recv,
           a_send, a_fsend, a_csend, a_recv, a_crecv,
           b_send, b_fsend, b_csend, b_recv, b_crecv,
           f_send, f_csend, f_recv, f_crecv,
           r_send, r_recv):
    tile = lax.axis_index("tile")
    z = lax.axis_index("aux")
    core = lax.rem(tile, 2)
    x = lax.rem(tile // 2, NX)
    y = tile // (2 * NX)
    pos = lax.rem(z, LINE)
    rank = z // LINE
    base = z - pos
    rows = b_ref.shape[0]
    ctiles = b_all.shape[0]
    nb = ctiles // (2 * NX)
    slot = (0, 1, 3, 2)

    def at(xx, yy, cc):
        return (yy * NX + xx) * 2 + cc

    def xp(i):
        return lax.rem(x + i, NX)

    def yp(i):
        return lax.rem(y + i, NY)

    def xdev(i):
        return (at(xp(i), y, core), z)

    def ydev(i):
        return (at(x, yp(i), core), z)

    def zdev(i):
        return (tile, lax.rem(z + LINE * i, LINE * QUAD))

    def ldev(i):
        return (tile, base + lax.rem(pos + i, LINE))

    sib = (at(x, y, 1 - core), z)
    mine = (tile * LINE * QUAD + base) * 2

    def remote(src, dst, ss, rs, dev):
        return pltpu.make_async_remote_copy(
            src_ref=src, dst_ref=dst, send_sem=ss, recv_sem=rs, device_id=dev, device_id_type=MESH)

    def signal(sem, dev):
        pl.semaphore_signal(sem, inc=1, device_id=dev, device_id_type=MESH)

    local = [
        pltpu.make_async_copy(a_ref, a_all.at[pl.ds(tile * 4, 4)], loc_sem.at[0]),
        pltpu.make_async_copy(col_ref, cols_v.at[pos], loc_sem.at[1]),
        pltpu.make_async_copy(tgt_ref, tgts_v.at[pos], loc_sem.at[2]),
        pltpu.make_async_copy(
            amp_ref.at[:, pl.ds(pl.multiple_of(mine - lax.rem(mine, 128), 128), 128)], amp_s, loc_sem.at[3]),
    ]
    for c in range(ctiles):
        local.append(pltpu.make_async_copy(
            b_ref.at[:, pl.ds(c * 128, 128)], b_all.at[c, pl.ds(0, rows)], loc_sem.at[6 + c]))

    barrier = pltpu.get_barrier_semaphore()
    near = [f(i) for i in (1, 2, 3) for f in (xdev, ydev)] + [sib]
    for dev in near:
        signal(barrier, dev)
    for i in (1, 2, 3):
        @pl.when(rank + i < QUAD)
        def _():
            signal(barrier, zdev(i))

        @pl.when(pos + i < LINE)
        def _():
            signal(barrier, ldev(i))
    for cp in local:
        cp.start()
    pl.semaphore_wait(barrier, len(near) + rank + pos)
    for i in (1, 2, 3):
        signal(p_ack, xdev(i))
    for i in (1, 2, 3):
        if i != 2:
            @pl.when(rank + i >= QUAD)
            def _():
                signal(z_ack.at[QUAD - i], zdev(i))

        @pl.when(pos + i >= LINE)
        def _():
            signal(l_ack.at[LINE - i], ldev(i))

    def zcopy(i):
        return remote(b_ref.at[:, pl.ds(pl.multiple_of(tile * 128, 128), 128)],
                      b_all.at[tile, pl.ds(rows * slot[QUAD - i], rows)],
                      z_send.at[i], z_recv.at[QUAD - i], zdev(i))

    def zwait(r):
        rows_r = b_all.at[tile, pl.ds(rows * slot[r], rows)]
        remote(rows_r, rows_r, z_send.at[r], z_recv.at[r], zdev(r)).wait_recv()

    def zup(i, ranks):
        for r in ranks:
            @pl.when(rank == r)
            def _():
                pl.semaphore_wait(z_ack.at[i], 1)

                @pl.when(y < nb)
                def _():
                    zcopy(i).start()

    def zpass(i, r):
        rows_r = b_all.at[tile, pl.ds(rows * slot[r], rows)]
        return remote(rows_r, b_all.at[tile, pl.ds(rows * slot[2], rows)], z_send.at[2], z_recv.at[2], zdev(i))

    def on_rank(r, f):
        @pl.when((rank == r) & (y < nb))
        def _():
            f()

    def relay():
        def one():
            zwait(3)
            zpass(1, 3).start()

        def zero():
            zwait(1)
            zpass(3, 1).start()

        on_rank(1, one)
        on_rank(0, zero)

    for i in (2, 1, 3):
        @pl.when((rank + i >= QUAD) & (y < nb))
        def _():
            zcopy(i).start()

    def lcopies(i):
        return [remote(v.at[pos], v.at[pos], l_send.at[n, i], l_recv.at[n, i], ldev(i))
                for n, v in enumerate((cols_v, tgts_v))]

    def lwaits(i):
        j = lax.rem(pos + i, LINE)
        for n, v in enumerate((cols_v, tgts_v)):
            remote(v.at[j], v.at[j], l_send.at[n, i], l_recv.at[n, LINE - i], ldev(i)).wait_recv()

    def apiece(d, h):
        return a_all.at[pl.ds(d * 4 + 2 * h, 2)]

    def whole(d):
        return a_all.at[pl.ds(d * 4, 4)]

    def asend(h, k, i, dev):
        return remote(a_ref.at[pl.ds(2 * h, 2)], apiece(tile, h), a_send.at[h, k, i], a_recv.at[h, tile // 2], dev)

    def acore(d):
        return remote(whole(d), whole(d), a_csend.at[d // 2], a_crecv.at[d // 2], sib)

    def await_a(d, h):
        remote(apiece(d, h), apiece(d, h), a_send.at[0, 0, 0], a_recv.at[h, d // 2], sib).wait_recv()

    def afwd(h, j, i, d, dev):
        return remote(apiece(d, h), apiece(d, h), a_fsend.at[h, j, i], a_recv.at[h, d // 2], dev)

    for i in (1, 3, 2):
        asend(0, 0, i, xdev(i)).start()
        asend(1, 1, i, ydev(i)).start()
    for i in (1, 3, 2):
        asend(0, 1, i, ydev(i)).start()
        asend(1, 0, i, xdev(i)).start()
    for cp in local[1:3]:
        cp.wait()
    for i in (1, 2, 3):
        @pl.when(pos + i >= LINE)
        def _():
            for cp in lcopies(i):
                cp.start()
    remote(a_ref, whole(tile), a_csend.at[tile // 2], a_crecv.at[tile // 2], sib).start()

    for j in (1, 3, 2):
        d = at(xp(j), y, core)
        await_a(d, 0)
        for i in (1, 3, 2):
            afwd(0, j, i, d, ydev(i)).start()
        d = at(x, yp(j), core)
        await_a(d, 1)
        for i in (1, 3, 2):
            afwd(1, j, i, d, xdev(i)).start()
        if j == 1:
            zup(1, (2,))

    zup(1, (0, 1))
    zup(3, (0,))
    relay()
    for i in (1, 2, 3):
        @pl.when(pos + i < LINE)
        def _():
            pl.semaphore_wait(l_ack.at[i], 1)
            for cp in lcopies(i):
                cp.start()

    def bpiece(d, h):
        return b_all.at[d, pl.ds(rows + rows * h, rows)]

    def bnear(d):
        return b_all.at[d, pl.ds(rows, 2 * rows)]

    def bfar(d):
        return b_all.at[d, pl.ds(3 * rows, rows)]

    def bsend(h, k, i, dev):
        return remote(bpiece(tile, h), bpiece(tile, h), b_send.at[h, k, i], b_recv.at[h, tile // 2], dev)

    def bcore(d):
        return remote(bnear(d), bnear(d), b_csend.at[d // 2], b_crecv.at[d // 2], sib)

    def await_b(d, h):
        remote(bpiece(d, h), bpiece(d, h), b_send.at[0, 0, 0], b_recv.at[h, d // 2], sib).wait_recv()

    def bfwd(h, j, i, d, dev):
        return remote(bpiece(d, h), bpiece(d, h), b_fsend.at[h, j, i], b_recv.at[h, d // 2], dev)

    def b_own():
        @pl.when(y < nb)
        def _():
            @pl.when(rank != 0)
            def _():
                zwait(1)

            @pl.when(rank != 1)
            def _():
                zwait(3)

            for i in (1, 3, 2):
                bsend(0, 0, i, xdev(i)).start()
                bsend(1, 1, i, ydev(i)).start()
            for i in (1, 3, 2):
                bsend(0, 1, i, ydev(i)).start()
                bsend(1, 0, i, xdev(i)).start()
            bcore(tile).start()

    def b_forward():
        for j in (1, 3, 2):
            @pl.when(y < nb)
            def _():
                d = at(xp(j), y, core)
                await_b(d, 0)
                for i in (1, 3, 2):
                    bfwd(0, j, i, d, ydev(i)).start()

            @pl.when(yp(j) < nb)
            def _():
                d = at(x, yp(j), core)
                await_b(d, 1)
                for i in (1, 3, 2):
                    bfwd(1, j, i, d, xdev(i)).start()

    def rest_b(yy, d, zero, one):
        @pl.when(yy < nb)
        def _():
            if zero:
                await_b(d, 0)
            if one:
                await_b(d, 1)
            bcore(d).start()

    def b_rest():
        for j in (1, 2, 3):
            rest_b(y, at(xp(j), y, core), False, True)
            rest_b(yp(j), at(x, yp(j), core), True, False)
        for i in (1, 2, 3):
            for j in (1, 2, 3):
                rest_b(yp(i), at(xp(j), yp(i), core), True, True)

    others = sorted(
        ((i, j) for i in range(NX) for j in range(NY) if i + j),
        key=lambda p: -min(p[0], NX - p[0]) - min(p[1], NY - p[1]))

    def fsend(i, j):
        return remote(bfar(tile), bfar(tile), f_send.at[NX * j + i], f_recv.at[tile // 2], (at(xp(i), yp(j), core), z))

    def fcore(d):
        return remote(bfar(d), bfar(d), f_csend.at[d // 2], f_crecv.at[d // 2], sib)

    def f_own():
        pl.semaphore_wait(p_ack, 3)

        @pl.when(y < nb)
        def _():
            zwait(2)
            for i, j in others:
                fsend(i, j).start()
            fcore(tile).start()

    def f_rest():
        for i, j in reversed(others):
            @pl.when(yp(j) < nb)
            def _():
                d = at(xp(i), yp(j), core)
                remote(bfar(d), bfar(d), f_send.at[0], f_recv.at[d // 2], sib).wait_recv()
                fcore(d).start()

    def rest_a(d, zero, one):
        if zero:
            await_a(d, 0)
        if one:
            await_a(d, 1)
        acore(d).start()

    b_own()
    for j in (1, 2, 3):
        rest_a(at(xp(j), y, core), False, True)
        rest_a(at(x, yp(j), core), True, False)

    @pl.when(rank == 0)
    def _():
        b_forward()

    f_own()

    @pl.when(rank != 0)
    def _():
        b_forward()

    for i in (1, 3, 2):
        for j in (1, 3, 2):
            rest_a(at(xp(j), yp(i), core), True, True)
    b_rest()
    for i in (1, 2, 3):
        lwaits(i)
    lists = [pltpu.make_async_copy(cols_v, cols_s, loc_sem.at[4]),
             pltpu.make_async_copy(tgts_v, tgts_s, loc_sem.at[5])]
    for cp in lists:
        cp.start()
    f_rest()

    def from_core_a(n, _):
        d = n * 2 + 1 - core
        remote(whole(d), whole(d), a_csend.at[n], a_crecv.at[n], sib).wait_recv()
        return 0

    lax.fori_loop(0, NX * NY, from_core_a, 0)

    def from_core_b(n, _):
        d = n * 2 + 1 - core
        remote(bnear(d), bnear(d), b_csend.at[n], b_crecv.at[n], sib).wait_recv()
        remote(bfar(d), bfar(d), f_csend.at[n], f_crecv.at[n], sib).wait_recv()
        return 0

    lax.fori_loop(0, nb * NX, from_core_b, 0)
    for cp in lists + local[:1] + local[3:]:
        cp.wait()

    def left(p, o):
        total = None
        for k in range(0, 16, 2):
            am = jnp.concatenate([a_all[amp_s[k + s, lax.rem(mine, 128) + 2 * p + o]] for s in (0, 1)], axis=1)
            bm = jnp.concatenate([b_all[cols_s[p, o, k + s]] for s in (0, 1)], axis=1)
            term = lax.dot_general(am, bm, NT, preferred_element_type=jnp.float32)
            total = term if total is None else total + term
        return total.astype(jnp.bfloat16)

    def partial(p):
        both = [left(p, o) for o in (0, 1)]
        return [lax.dot_general(both[o], b_all[tgts_s[p, 0, o]], NN, preferred_element_type=jnp.float32) for o in (0, 1)]

    def rcopy(i, o):
        n = (i - 1) * 2 + o
        return remote(part_s.at[n], part_r.at[n], r_send.at[n], r_recv.at[n], ldev(i))

    upper = pos // 2
    for dest in (3 * (1 - upper), 2 - upper, pos + 1 - 2 * lax.rem(pos, 2)):
        i = lax.rem(dest - pos + LINE, LINE)
        for o, r in enumerate(partial(dest)):
            part_s[2 * i - 2 + o] = r.astype(jnp.bfloat16)
            rcopy(i, o).start()
    for o, r in enumerate(partial(pos)):
        own[o] = r

    for i in (1, 2, 3):
        for o in (0, 1):
            rcopy(i, o).wait_recv()
    for o in range(2):
        out_ref[o] = (own[o] + part_r[o].astype(jnp.float32) + part_r[2 + o].astype(jnp.float32)
                      + part_r[4 + o].astype(jnp.float32)).astype(jnp.bfloat16)

    for i in (1, 2, 3):
        for o in (0, 1):
            rcopy(i, o).wait_send()
        for cp in lcopies(i):
            cp.wait_send()
        for h in (0, 1):
            asend(h, 0, i, xdev(i)).wait_send()
            asend(h, 1, i, ydev(i)).wait_send()
        for j in (1, 2, 3):
            afwd(0, j, i, at(xp(j), y, core), ydev(i)).wait_send()
            afwd(1, j, i, at(x, yp(j), core), xdev(i)).wait_send()

    def core_sent(n, _):
        acore(n * 2 + core).wait_send()
        return 0

    lax.fori_loop(0, NX * NY, core_sent, 0)

    def bcore_sent(n, _):
        bcore(n * 2 + core).wait_send()
        fcore(n * 2 + core).wait_send()
        return 0

    lax.fori_loop(0, nb * NX, bcore_sent, 0)

    @pl.when(y < nb)
    def _():
        for i, j in others:
            fsend(i, j).wait_send()
        for i in (1, 2, 3):
            zcopy(i).wait_send()
            for h in (0, 1):
                bsend(h, 0, i, xdev(i)).wait_send()
                bsend(h, 1, i, ydev(i)).wait_send()
            for j in (1, 2, 3):
                bfwd(0, j, i, at(xp(j), y, core), ydev(i)).wait_send()

    for j in (1, 2, 3):
        @pl.when(yp(j) < nb)
        def _():
            for i in (1, 2, 3):
                bfwd(1, j, i, at(x, yp(j), core), xdev(i)).wait_send()


def body(amplitudes, df_factors, out_tiles, pair_col, pair_amp):
    ts = amplitudes.shape[1]
    rows, cols = df_factors.shape
    ctiles = cols // ts
    pairs = pair_col.shape[1]
    dma = pltpu.SemaphoreType.DMA
    reg = pltpu.SemaphoreType.REGULAR
    chips = NX * NY
    anyw = pl.BlockSpec(memory_space=pl.ANY)
    return pl.pallas_call(
        kernel,
        out_shape=jax.ShapeDtypeStruct((2, ts, ts), jnp.bfloat16),
        in_specs=[anyw] * 5,
        out_specs=pl.BlockSpec(memory_space=pltpu.VMEM),
        scratch_shapes=[
            pltpu.VMEM((4 * 2 * chips, ts, ts), jnp.bfloat16),
            pltpu.VMEM((ctiles, QUAD * rows, ts), jnp.bfloat16),
            pltpu.VMEM((LINE, 2, pairs), jnp.int32),
            pltpu.VMEM((LINE, 1, 2), jnp.int32),
            pltpu.SMEM((pairs, 128), jnp.int32),
            pltpu.SMEM((LINE, 2, pairs), jnp.int32),
            pltpu.SMEM((LINE, 1, 2), jnp.int32),
            pltpu.VMEM((2, ts, ts), jnp.float32),
            pltpu.VMEM((6, ts, ts), jnp.bfloat16),
            pltpu.VMEM((6, ts, ts), jnp.bfloat16),
            dma((6 + ctiles,)), reg, reg((4,)), reg((4,)), dma((4,)), dma((4,)), dma((2, 4)), dma((2, 4)),
            dma((2, 2, 4)), dma((2, 4, 4)), dma((chips,)), dma((2, chips)), dma((chips,)),
            dma((2, 2, 4)), dma((2, 4, 4)), dma((chips,)), dma((2, chips)), dma((chips,)),
            dma((chips,)), dma((chips,)), dma((chips,)), dma((chips,)),
            dma((6,)), dma((6,)),
        ],
        compiler_params=pltpu.CompilerParams(
            collective_id=0, has_side_effects=True, vmem_limit_bytes=56 * 2**20),
        name="residual",
    )(pair_amp.T, pair_col, out_tiles[None], amplitudes, df_factors)


def solution(mesh):
    in_specs = (
        P("tile", None, None),
        P("aux", None),
        P(("tile", "aux")),
        P(("tile", "aux"), None),
        P(),
    )
    out_specs = P(("tile", "aux"), None, None)
    return jax.shard_map(body, mesh=mesh, in_specs=in_specs, out_specs=out_specs, check_vma=False)
```

```python
import functools

import jax
import jax.numpy as jnp
from jax import lax
from jax.experimental import pallas as pl
from jax.experimental.pallas import tpu as pltpu
from jax.sharding import PartitionSpec as P

MESH = pl.DeviceIdType.MESH
NX = 4
NY = 4
LINE = 4
QUAD = 4
NT = (((1,), (1,)), ((), ()))
NN = (((1,), (0,)), ((), ()))


def kernel(amp_ref, col_ref, tgt_ref, a_ref, b_ref, out_ref,
           a_all, b_all, cols_v, tgts_v, amp_s, cols_s, tgts_s, own, part_s, part_r,
           loc_sem, p_ack, z_ack, l_ack, z_send, z_recv, l_send, l_recv,
           a_send, a_fsend, a_csend, a_recv, a_crecv,
           b_send, b_fsend, b_csend, b_recv, b_crecv,
           f_send, f_csend, f_recv, f_crecv,
           r_send, r_recv):
    tile = lax.axis_index("tile")
    z = lax.axis_index("aux")
    core = lax.rem(tile, 2)
    x = lax.rem(tile // 2, NX)
    y = tile // (2 * NX)
    pos = lax.rem(z, LINE)
    rank = z // LINE
    base = z - pos
    rows = b_ref.shape[0]
    ctiles = b_all.shape[0]
    nb = ctiles // (2 * NX)
    slot = (0, 1, 3, 2)

    def at(xx, yy, cc):
        return (yy * NX + xx) * 2 + cc

    def xp(i):
        return lax.rem(x + i, NX)

    def yp(i):
        return lax.rem(y + i, NY)

    def xdev(i):
        return (at(xp(i), y, core), z)

    def ydev(i):
        return (at(x, yp(i), core), z)

    def zdev(i):
        return (tile, lax.rem(z + LINE * i, LINE * QUAD))

    def ldev(i):
        return (tile, base + lax.rem(pos + i, LINE))

    sib = (at(x, y, 1 - core), z)
    mine = (tile * LINE * QUAD + base) * 2

    def remote(src, dst, ss, rs, dev):
        return pltpu.make_async_remote_copy(
            src_ref=src, dst_ref=dst, send_sem=ss, recv_sem=rs, device_id=dev, device_id_type=MESH)

    def signal(sem, dev):
        pl.semaphore_signal(sem, inc=1, device_id=dev, device_id_type=MESH)

    local = [
        pltpu.make_async_copy(a_ref, a_all.at[pl.ds(tile * 4, 4)], loc_sem.at[0]),
        pltpu.make_async_copy(col_ref, cols_v.at[pos], loc_sem.at[1]),
        pltpu.make_async_copy(tgt_ref, tgts_v.at[pos], loc_sem.at[2]),
        pltpu.make_async_copy(
            amp_ref.at[:, pl.ds(pl.multiple_of(mine - lax.rem(mine, 128), 128), 128)], amp_s, loc_sem.at[3]),
    ]
    for c in range(ctiles):
        local.append(pltpu.make_async_copy(
            b_ref.at[:, pl.ds(c * 128, 128)], b_all.at[c, pl.ds(0, rows)], loc_sem.at[6 + c]))

    barrier = pltpu.get_barrier_semaphore()
    near = [f(i) for i in (1, 2, 3) for f in (xdev, ydev)] + [sib]
    for dev in near:
        signal(barrier, dev)
    for i in (1, 2, 3):
        @pl.when(rank + i < QUAD)
        def _():
            signal(barrier, zdev(i))

        @pl.when(pos + i < LINE)
        def _():
            signal(barrier, ldev(i))
    for cp in local:
        cp.start()
    pl.semaphore_wait(barrier, len(near) + rank + pos)
    for i in (1, 2, 3):
        signal(p_ack, xdev(i))
    for i in (1, 2, 3):
        if i != 2:
            @pl.when(rank + i >= QUAD)
            def _():
                signal(z_ack.at[QUAD - i], zdev(i))

        @pl.when(pos + i >= LINE)
        def _():
            signal(l_ack.at[LINE - i], ldev(i))

    def zcopy(i):
        return remote(b_ref.at[:, pl.ds(pl.multiple_of(tile * 128, 128), 128)],
                      b_all.at[tile, pl.ds(rows * slot[QUAD - i], rows)],
                      z_send.at[i], z_recv.at[QUAD - i], zdev(i))

    def zwait(r):
        rows_r = b_all.at[tile, pl.ds(rows * slot[r], rows)]
        remote(rows_r, rows_r, z_send.at[r], z_recv.at[r], zdev(r)).wait_recv()

    def zup(i, ranks):
        for r in ranks:
            @pl.when(rank == r)
            def _():
                pl.semaphore_wait(z_ack.at[i], 1)

                @pl.when(y < nb)
                def _():
                    zcopy(i).start()

    def zpass(i, r):
        rows_r = b_all.at[tile, pl.ds(rows * slot[r], rows)]
        return remote(rows_r, b_all.at[tile, pl.ds(rows * slot[2], rows)], z_send.at[2], z_recv.at[2], zdev(i))

    def on_rank(r, f):
        @pl.when((rank == r) & (y < nb))
        def _():
            f()

    def relay():
        def one():
            zwait(3)
            zpass(1, 3).start()

        def zero():
            zwait(1)
            zpass(3, 1).start()

        on_rank(1, one)
        on_rank(0, zero)

    for i in (2, 1, 3):
        @pl.when((rank + i >= QUAD) & (y < nb))
        def _():
            zcopy(i).start()

    def lcopies(i):
        return [remote(v.at[pos], v.at[pos], l_send.at[n, i], l_recv.at[n, i], ldev(i))
                for n, v in enumerate((cols_v, tgts_v))]

    def lwaits(i):
        j = lax.rem(pos + i, LINE)
        for n, v in enumerate((cols_v, tgts_v)):
            remote(v.at[j], v.at[j], l_send.at[n, i], l_recv.at[n, LINE - i], ldev(i)).wait_recv()

    def apiece(d, h):
        return a_all.at[pl.ds(d * 4 + 2 * h, 2)]

    def whole(d):
        return a_all.at[pl.ds(d * 4, 4)]

    def asend(h, k, i, dev):
        return remote(a_ref.at[pl.ds(2 * h, 2)], apiece(tile, h), a_send.at[h, k, i], a_recv.at[h, tile // 2], dev)

    def acore(d):
        return remote(whole(d), whole(d), a_csend.at[d // 2], a_crecv.at[d // 2], sib)

    def await_a(d, h):
        remote(apiece(d, h), apiece(d, h), a_send.at[0, 0, 0], a_recv.at[h, d // 2], sib).wait_recv()

    def afwd(h, j, i, d, dev):
        return remote(apiece(d, h), apiece(d, h), a_fsend.at[h, j, i], a_recv.at[h, d // 2], dev)

    for i in (1, 3, 2):
        asend(0, 0, i, xdev(i)).start()
        asend(1, 1, i, ydev(i)).start()
    for i in (1, 3, 2):
        asend(0, 1, i, ydev(i)).start()
        asend(1, 0, i, xdev(i)).start()
    for cp in local[1:3]:
        cp.wait()
    for i in (1, 2, 3):
        @pl.when(pos + i >= LINE)
        def _():
            for cp in lcopies(i):
                cp.start()
    remote(a_ref, whole(tile), a_csend.at[tile // 2], a_crecv.at[tile // 2], sib).start()

    for j in (1, 3, 2):
        d = at(xp(j), y, core)
        await_a(d, 0)
        for i in (1, 3, 2):
            afwd(0, j, i, d, ydev(i)).start()
        d = at(x, yp(j), core)
        await_a(d, 1)
        for i in (1, 3, 2):
            afwd(1, j, i, d, xdev(i)).start()
        if j == 1:
            zup(1, (2,))

    zup(1, (0, 1))
    zup(3, (0,))
    relay()
    for i in (1, 2, 3):
        @pl.when(pos + i < LINE)
        def _():
            pl.semaphore_wait(l_ack.at[i], 1)
            for cp in lcopies(i):
                cp.start()

    def bpiece(d, h):
        return b_all.at[d, pl.ds(rows + rows * h, rows)]

    def bnear(d):
        return b_all.at[d, pl.ds(rows, 2 * rows)]

    def bfar(d):
        return b_all.at[d, pl.ds(3 * rows, rows)]

    def bsend(h, k, i, dev):
        return remote(bpiece(tile, h), bpiece(tile, h), b_send.at[h, k, i], b_recv.at[h, tile // 2], dev)

    def bcore(d):
        return remote(bnear(d), bnear(d), b_csend.at[d // 2], b_crecv.at[d // 2], sib)

    def await_b(d, h):
        remote(bpiece(d, h), bpiece(d, h), b_send.at[0, 0, 0], b_recv.at[h, d // 2], sib).wait_recv()

    def bfwd(h, j, i, d, dev):
        return remote(bpiece(d, h), bpiece(d, h), b_fsend.at[h, j, i], b_recv.at[h, d // 2], dev)

    def b_own():
        @pl.when(y < nb)
        def _():
            @pl.when(rank != 0)
            def _():
                zwait(1)

            @pl.when(rank != 1)
            def _():
                zwait(3)

            for i in (1, 3, 2):
                bsend(0, 0, i, xdev(i)).start()
                bsend(1, 1, i, ydev(i)).start()
            for i in (1, 3, 2):
                bsend(0, 1, i, ydev(i)).start()
                bsend(1, 0, i, xdev(i)).start()
            bcore(tile).start()

    def b_forward():
        for j in (1, 3, 2):
            @pl.when(y < nb)
            def _():
                d = at(xp(j), y, core)
                await_b(d, 0)
                for i in (1, 3, 2):
                    bfwd(0, j, i, d, ydev(i)).start()

            @pl.when(yp(j) < nb)
            def _():
                d = at(x, yp(j), core)
                await_b(d, 1)
                for i in (1, 3, 2):
                    bfwd(1, j, i, d, xdev(i)).start()

    def rest_b(yy, d, zero, one):
        @pl.when(yy < nb)
        def _():
            if zero:
                await_b(d, 0)
            if one:
                await_b(d, 1)
            bcore(d).start()

    def b_rest():
        for j in (1, 2, 3):
            rest_b(y, at(xp(j), y, core), False, True)
            rest_b(yp(j), at(x, yp(j), core), True, False)
        for i in (1, 2, 3):
            for j in (1, 2, 3):
                rest_b(yp(i), at(xp(j), yp(i), core), True, True)

    others = sorted(
        ((i, j) for i in range(NX) for j in range(NY) if i + j),
        key=lambda p: -min(p[0], NX - p[0]) - min(p[1], NY - p[1]))

    def fsend(i, j):
        return remote(bfar(tile), bfar(tile), f_send.at[NX * j + i], f_recv.at[tile // 2], (at(xp(i), yp(j), core), z))

    def fcore(d):
        return remote(bfar(d), bfar(d), f_csend.at[d // 2], f_crecv.at[d // 2], sib)

    def f_own():
        pl.semaphore_wait(p_ack, 3)

        @pl.when(y < nb)
        def _():
            zwait(2)
            for i, j in others:
                fsend(i, j).start()
            fcore(tile).start()

    def f_rest():
        for i, j in reversed(others):
            @pl.when(yp(j) < nb)
            def _():
                d = at(xp(i), yp(j), core)
                remote(bfar(d), bfar(d), f_send.at[0], f_recv.at[d // 2], sib).wait_recv()
                fcore(d).start()

    def rest_a(d, zero, one):
        if zero:
            await_a(d, 0)
        if one:
            await_a(d, 1)
        acore(d).start()

    b_own()
    for j in (1, 2, 3):
        rest_a(at(xp(j), y, core), False, True)
        rest_a(at(x, yp(j), core), True, False)

    @pl.when(rank == 0)
    def _():
        b_forward()

    f_own()

    @pl.when(rank != 0)
    def _():
        b_forward()

    for i in (1, 3, 2):
        for j in (1, 3, 2):
            rest_a(at(xp(j), yp(i), core), True, True)
    b_rest()
    for i in (1, 2, 3):
        lwaits(i)
    lists = [pltpu.make_async_copy(cols_v, cols_s, loc_sem.at[4]),
             pltpu.make_async_copy(tgts_v, tgts_s, loc_sem.at[5])]
    for cp in lists:
        cp.start()
    f_rest()

    def from_core_a(n, _):
        d = n * 2 + 1 - core
        remote(whole(d), whole(d), a_csend.at[n], a_crecv.at[n], sib).wait_recv()
        return 0

    lax.fori_loop(0, NX * NY, from_core_a, 0)

    def from_core_b(n, _):
        d = n * 2 + 1 - core
        remote(bnear(d), bnear(d), b_csend.at[n], b_crecv.at[n], sib).wait_recv()
        remote(bfar(d), bfar(d), f_csend.at[n], f_crecv.at[n], sib).wait_recv()
        return 0

    lax.fori_loop(0, nb * NX, from_core_b, 0)
    for cp in lists + local[:1] + local[3:]:
        cp.wait()

    def left(p, o):
        total = None
        for k in range(0, 16, 2):
            am = jnp.concatenate([a_all[amp_s[k + s, lax.rem(mine, 128) + 2 * p + o]] for s in (0, 1)], axis=1)
            bm = jnp.concatenate([b_all[cols_s[p, o, k + s]] for s in (0, 1)], axis=1)
            term = lax.dot_general(am, bm, NT, preferred_element_type=jnp.float32)
            total = term if total is None else total + term
        return total.astype(jnp.bfloat16)

    def partial(p):
        both = [left(p, o) for o in (0, 1)]
        return [lax.dot_general(both[o], b_all[tgts_s[p, 0, o]], NN, preferred_element_type=jnp.float32) for o in (0, 1)]

    def rcopy(i, o):
        n = (i - 1) * 2 + o
        return remote(part_s.at[n], part_r.at[n], r_send.at[n], r_recv.at[n], ldev(i))

    upper = pos // 2

    def one_dest(n, _):
        last = n // 3
        third = n // 2 - last
        second = lax.rem(n, 2) - last
        dest = ((1 - second - third - last) * 3 * (1 - upper) + second * (2 - upper)
                + third * (pos + 1 - 2 * lax.rem(pos, 2)) + last * pos)
        i = lax.rem(dest - pos + LINE, LINE)
        both = partial(dest)

        @pl.when(n < LINE - 1)
        def _():
            for o, r in enumerate(both):
                part_s[2 * i - 2 + o] = r.astype(jnp.bfloat16)
                rcopy(i, o).start()

        @pl.when(n == LINE - 1)
        def _():
            for o, r in enumerate(both):
                own[o] = r

        return 0

    lax.fori_loop(0, LINE, one_dest, 0)

    for i in (1, 2, 3):
        for o in (0, 1):
            rcopy(i, o).wait_recv()
    for o in range(2):
        out_ref[o] = (own[o] + part_r[o].astype(jnp.float32) + part_r[2 + o].astype(jnp.float32)
                      + part_r[4 + o].astype(jnp.float32)).astype(jnp.bfloat16)

    for i in (1, 2, 3):
        for o in (0, 1):
            rcopy(i, o).wait_send()
        for cp in lcopies(i):
            cp.wait_send()
        for h in (0, 1):
            asend(h, 0, i, xdev(i)).wait_send()
            asend(h, 1, i, ydev(i)).wait_send()
        for j in (1, 2, 3):
            afwd(0, j, i, at(xp(j), y, core), ydev(i)).wait_send()
            afwd(1, j, i, at(x, yp(j), core), xdev(i)).wait_send()

    def core_sent(n, _):
        acore(n * 2 + core).wait_send()
        return 0

    lax.fori_loop(0, NX * NY, core_sent, 0)

    def bcore_sent(n, _):
        bcore(n * 2 + core).wait_send()
        fcore(n * 2 + core).wait_send()
        return 0

    lax.fori_loop(0, nb * NX, bcore_sent, 0)

    @pl.when(y < nb)
    def _():
        for i, j in others:
            fsend(i, j).wait_send()
        for i in (1, 2, 3):
            zcopy(i).wait_send()
            for h in (0, 1):
                bsend(h, 0, i, xdev(i)).wait_send()
                bsend(h, 1, i, ydev(i)).wait_send()
            for j in (1, 2, 3):
                bfwd(0, j, i, at(xp(j), y, core), ydev(i)).wait_send()

    for j in (1, 2, 3):
        @pl.when(yp(j) < nb)
        def _():
            for i in (1, 2, 3):
                bfwd(1, j, i, at(x, yp(j), core), xdev(i)).wait_send()


def body(amplitudes, df_factors, out_tiles, pair_col, pair_amp):
    ts = amplitudes.shape[1]
    rows, cols = df_factors.shape
    ctiles = cols // ts
    pairs = pair_col.shape[1]
    dma = pltpu.SemaphoreType.DMA
    reg = pltpu.SemaphoreType.REGULAR
    chips = NX * NY
    anyw = pl.BlockSpec(memory_space=pl.ANY)
    return pl.pallas_call(
        kernel,
        out_shape=jax.ShapeDtypeStruct((2, ts, ts), jnp.bfloat16),
        in_specs=[anyw] * 5,
        out_specs=pl.BlockSpec(memory_space=pltpu.VMEM),
        scratch_shapes=[
            pltpu.VMEM((4 * 2 * chips, ts, ts), jnp.bfloat16),
            pltpu.VMEM((ctiles, QUAD * rows, ts), jnp.bfloat16),
            pltpu.VMEM((LINE, 2, pairs), jnp.int32),
            pltpu.VMEM((LINE, 1, 2), jnp.int32),
            pltpu.SMEM((pairs, 128), jnp.int32),
            pltpu.SMEM((LINE, 2, pairs), jnp.int32),
            pltpu.SMEM((LINE, 1, 2), jnp.int32),
            pltpu.VMEM((2, ts, ts), jnp.float32),
            pltpu.VMEM((6, ts, ts), jnp.bfloat16),
            pltpu.VMEM((6, ts, ts), jnp.bfloat16),
            dma((6 + ctiles,)), reg, reg((4,)), reg((4,)), dma((4,)), dma((4,)), dma((2, 4)), dma((2, 4)),
            dma((2, 2, 4)), dma((2, 4, 4)), dma((chips,)), dma((2, chips)), dma((chips,)),
            dma((2, 2, 4)), dma((2, 4, 4)), dma((chips,)), dma((2, chips)), dma((chips,)),
            dma((chips,)), dma((chips,)), dma((chips,)), dma((chips,)),
            dma((6,)), dma((6,)),
        ],
        compiler_params=pltpu.CompilerParams(
            collective_id=0, has_side_effects=True, vmem_limit_bytes=861 * 2**16),
        name="residual",
    )(pair_amp.T, pair_col, out_tiles[None], amplitudes, df_factors)


def solution(mesh):
    in_specs = (
        P("tile", None, None),
        P("aux", None),
        P(("tile", "aux")),
        P(("tile", "aux"), None),
        P(),
    )
    out_specs = P(("tile", "aux"), None, None)
    return jax.shard_map(body, mesh=mesh, in_specs=in_specs, out_specs=out_specs, check_vma=False)
```

```python
import functools

import jax
import jax.numpy as jnp
from jax import lax
from jax.experimental import pallas as pl
from jax.experimental.pallas import tpu as pltpu
from jax.sharding import PartitionSpec as P

MESH = pl.DeviceIdType.MESH
NX = 4
NY = 4
LINE = 4
QUAD = 4
NT = (((1,), (1,)), ((), ()))
NN = (((1,), (0,)), ((), ()))


def kernel(amp_ref, col_ref, tgt_ref, a_ref, b_ref, out_ref,
           a_all, b_all, cols_v, tgts_v, amp_s, cols_s, tgts_s, own, part_s, part_r,
           loc_sem, p_ack, z_ack, l_ack, z_send, z_recv, l_send, l_recv,
           a_send, a_fsend, a_csend, a_recv, a_crecv,
           b_send, b_fsend, b_csend, b_recv, b_crecv,
           f_send, f_csend, f_recv, f_crecv,
           r_send, r_recv):
    tile = lax.axis_index("tile")
    z = lax.axis_index("aux")
    core = lax.rem(tile, 2)
    x = lax.rem(tile // 2, NX)
    y = tile // (2 * NX)
    pos = lax.rem(z, LINE)
    rank = z // LINE
    base = z - pos
    rows = b_ref.shape[0]
    ctiles = b_all.shape[0]
    nb = ctiles // (2 * NX)
    slot = (0, 1, 3, 2)

    def at(xx, yy, cc):
        return (yy * NX + xx) * 2 + cc

    def xp(i):
        return lax.rem(x + i, NX)

    def yp(i):
        return lax.rem(y + i, NY)

    def xdev(i):
        return (at(xp(i), y, core), z)

    def ydev(i):
        return (at(x, yp(i), core), z)

    def zdev(i):
        return (tile, lax.rem(z + LINE * i, LINE * QUAD))

    def ldev(i):
        return (tile, base + lax.rem(pos + i, LINE))

    sib = (at(x, y, 1 - core), z)
    mine = (tile * LINE * QUAD + base) * 2

    def remote(src, dst, ss, rs, dev):
        return pltpu.make_async_remote_copy(
            src_ref=src, dst_ref=dst, send_sem=ss, recv_sem=rs, device_id=dev, device_id_type=MESH)

    def signal(sem, dev):
        pl.semaphore_signal(sem, inc=1, device_id=dev, device_id_type=MESH)

    local = [
        pltpu.make_async_copy(a_ref, a_all.at[pl.ds(tile * 4, 4)], loc_sem.at[0]),
        pltpu.make_async_copy(col_ref, cols_v.at[pos], loc_sem.at[1]),
        pltpu.make_async_copy(tgt_ref, tgts_v.at[pos], loc_sem.at[2]),
        pltpu.make_async_copy(
            amp_ref.at[:, pl.ds(pl.multiple_of(mine - lax.rem(mine, 128), 128), 128)], amp_s, loc_sem.at[3]),
    ]
    for c in range(ctiles):
        local.append(pltpu.make_async_copy(
            b_ref.at[:, pl.ds(c * 128, 128)], b_all.at[c, pl.ds(0, rows)], loc_sem.at[6 + c]))

    barrier = pltpu.get_barrier_semaphore()
    near = [f(i) for i in (1, 2, 3) for f in (xdev, ydev)] + [sib]
    for dev in near:
        signal(barrier, dev)
    for i in (1, 2, 3):
        @pl.when(rank + i < QUAD)
        def _():
            signal(barrier, zdev(i))

        @pl.when(pos + i < LINE)
        def _():
            signal(barrier, ldev(i))
    for cp in local:
        cp.start()
    pl.semaphore_wait(barrier, len(near) + rank + pos)
    for i in (1, 2, 3):
        signal(p_ack, xdev(i))
    for i in (1, 2, 3):
        if i != 2:
            @pl.when(rank + i >= QUAD)
            def _():
                signal(z_ack.at[QUAD - i], zdev(i))

        @pl.when(pos + i >= LINE)
        def _():
            signal(l_ack.at[LINE - i], ldev(i))

    def zcopy(i):
        return remote(b_ref.at[:, pl.ds(pl.multiple_of(tile * 128, 128), 128)],
                      b_all.at[tile, pl.ds(rows * slot[QUAD - i], rows)],
                      z_send.at[i], z_recv.at[QUAD - i], zdev(i))

    def zwait(r):
        rows_r = b_all.at[tile, pl.ds(rows * slot[r], rows)]
        remote(rows_r, rows_r, z_send.at[r], z_recv.at[r], zdev(r)).wait_recv()

    def zup(i, ranks):
        for r in ranks:
            @pl.when(rank == r)
            def _():
                pl.semaphore_wait(z_ack.at[i], 1)

                @pl.when(y < nb)
                def _():
                    zcopy(i).start()

    def zpass(i, r):
        rows_r = b_all.at[tile, pl.ds(rows * slot[r], rows)]
        return remote(rows_r, b_all.at[tile, pl.ds(rows * slot[2], rows)], z_send.at[2], z_recv.at[2], zdev(i))

    def on_rank(r, f):
        @pl.when((rank == r) & (y < nb))
        def _():
            f()

    def relay():
        def one():
            zwait(3)
            zpass(1, 3).start()

        def zero():
            zwait(1)
            zpass(3, 1).start()

        on_rank(1, one)
        on_rank(0, zero)

    for i in (2, 1, 3):
        @pl.when((rank + i >= QUAD) & (y < nb))
        def _():
            zcopy(i).start()

    def lcopies(i):
        return [remote(v.at[pos], v.at[pos], l_send.at[n, i], l_recv.at[n, i], ldev(i))
                for n, v in enumerate((cols_v, tgts_v))]

    def lwaits(i):
        j = lax.rem(pos + i, LINE)
        for n, v in enumerate((cols_v, tgts_v)):
            remote(v.at[j], v.at[j], l_send.at[n, i], l_recv.at[n, LINE - i], ldev(i)).wait_recv()

    def apiece(d, h):
        return a_all.at[pl.ds(d * 4 + 2 * h, 2)]

    def whole(d):
        return a_all.at[pl.ds(d * 4, 4)]

    def asend(h, k, i, dev):
        return remote(a_ref.at[pl.ds(2 * h, 2)], apiece(tile, h), a_send.at[h, k, i], a_recv.at[h, tile // 2], dev)

    def acore(d):
        return remote(whole(d), whole(d), a_csend.at[d // 2], a_crecv.at[d // 2], sib)

    def await_a(d, h):
        remote(apiece(d, h), apiece(d, h), a_send.at[0, 0, 0], a_recv.at[h, d // 2], sib).wait_recv()

    def afwd(h, j, i, d, dev):
        return remote(apiece(d, h), apiece(d, h), a_fsend.at[h, j, i], a_recv.at[h, d // 2], dev)

    for i in (1, 3, 2):
        asend(0, 0, i, xdev(i)).start()
        asend(1, 1, i, ydev(i)).start()
    for i in (1, 3, 2):
        asend(0, 1, i, ydev(i)).start()
        asend(1, 0, i, xdev(i)).start()
    for cp in local[1:3]:
        cp.wait()
    for i in (1, 2, 3):
        @pl.when(pos + i >= LINE)
        def _():
            for cp in lcopies(i):
                cp.start()
    remote(a_ref, whole(tile), a_csend.at[tile // 2], a_crecv.at[tile // 2], sib).start()

    for j in (1, 3, 2):
        d = at(xp(j), y, core)
        await_a(d, 0)
        for i in (1, 3, 2):
            afwd(0, j, i, d, ydev(i)).start()
        d = at(x, yp(j), core)
        await_a(d, 1)
        for i in (1, 3, 2):
            afwd(1, j, i, d, xdev(i)).start()
        if j == 1:
            zup(1, (2,))

    zup(1, (0, 1))
    zup(3, (0,))
    relay()
    for i in (1, 2, 3):
        @pl.when(pos + i < LINE)
        def _():
            pl.semaphore_wait(l_ack.at[i], 1)
            for cp in lcopies(i):
                cp.start()

    def bpiece(d, h):
        return b_all.at[d, pl.ds(rows + rows * h, rows)]

    def bnear(d):
        return b_all.at[d, pl.ds(rows, 2 * rows)]

    def bfar(d):
        return b_all.at[d, pl.ds(3 * rows, rows)]

    def bsend(h, k, i, dev):
        return remote(bpiece(tile, h), bpiece(tile, h), b_send.at[h, k, i], b_recv.at[h, tile // 2], dev)

    def bcore(d):
        return remote(bnear(d), bnear(d), b_csend.at[d // 2], b_crecv.at[d // 2], sib)

    def await_b(d, h):
        remote(bpiece(d, h), bpiece(d, h), b_send.at[0, 0, 0], b_recv.at[h, d // 2], sib).wait_recv()

    def bfwd(h, j, i, d, dev):
        return remote(bpiece(d, h), bpiece(d, h), b_fsend.at[h, j, i], b_recv.at[h, d // 2], dev)

    def b_own():
        @pl.when(y < nb)
        def _():
            @pl.when(rank != 0)
            def _():
                zwait(1)

            @pl.when(rank != 1)
            def _():
                zwait(3)

            for i in (1, 3, 2):
                bsend(0, 0, i, xdev(i)).start()
                bsend(1, 1, i, ydev(i)).start()
            for i in (1, 3, 2):
                bsend(0, 1, i, ydev(i)).start()
                bsend(1, 0, i, xdev(i)).start()
            bcore(tile).start()

    def b_forward():
        for j in (1, 3, 2):
            @pl.when(y < nb)
            def _():
                d = at(xp(j), y, core)
                await_b(d, 0)
                for i in (1, 3, 2):
                    bfwd(0, j, i, d, ydev(i)).start()

            @pl.when(yp(j) < nb)
            def _():
                d = at(x, yp(j), core)
                await_b(d, 1)
                for i in (1, 3, 2):
                    bfwd(1, j, i, d, xdev(i)).start()

    def rest_b(yy, d, zero, one):
        @pl.when(yy < nb)
        def _():
            if zero:
                await_b(d, 0)
            if one:
                await_b(d, 1)
            bcore(d).start()

    def b_rest():
        for j in (1, 2, 3):
            rest_b(y, at(xp(j), y, core), False, True)
            rest_b(yp(j), at(x, yp(j), core), True, False)
        for i in (1, 2, 3):
            for j in (1, 2, 3):
                rest_b(yp(i), at(xp(j), yp(i), core), True, True)

    others = sorted(
        ((i, j) for i in range(NX) for j in range(NY) if i + j),
        key=lambda p: -min(p[0], NX - p[0]) - min(p[1], NY - p[1]))

    def fsend(i, j):
        return remote(bfar(tile), bfar(tile), f_send.at[NX * j + i], f_recv.at[tile // 2], (at(xp(i), yp(j), core), z))

    def fcore(d):
        return remote(bfar(d), bfar(d), f_csend.at[d // 2], f_crecv.at[d // 2], sib)

    def f_own():
        pl.semaphore_wait(p_ack, 3)

        @pl.when(y < nb)
        def _():
            zwait(2)
            for i, j in others:
                fsend(i, j).start()
            fcore(tile).start()

    def f_rest():
        for i, j in reversed(others):
            @pl.when(yp(j) < nb)
            def _():
                d = at(xp(i), yp(j), core)
                remote(bfar(d), bfar(d), f_send.at[0], f_recv.at[d // 2], sib).wait_recv()
                fcore(d).start()

    def rest_a(d, zero, one):
        if zero:
            await_a(d, 0)
        if one:
            await_a(d, 1)
        acore(d).start()

    b_own()
    for j in (1, 2, 3):
        rest_a(at(xp(j), y, core), False, True)
        rest_a(at(x, yp(j), core), True, False)

    @pl.when(rank == 0)
    def _():
        b_forward()

    f_own()

    @pl.when(rank != 0)
    def _():
        b_forward()

    for i in (1, 3, 2):
        for j in (1, 3, 2):
            rest_a(at(xp(j), yp(i), core), True, True)
    b_rest()
    for i in (1, 2, 3):
        lwaits(i)
    lists = [pltpu.make_async_copy(cols_v, cols_s, loc_sem.at[4]),
             pltpu.make_async_copy(tgts_v, tgts_s, loc_sem.at[5])]
    for cp in lists:
        cp.start()
    f_rest()

    def from_core_a(n, _):
        d = n * 2 + 1 - core
        remote(whole(d), whole(d), a_csend.at[n], a_crecv.at[n], sib).wait_recv()
        return 0

    lax.fori_loop(0, NX * NY, from_core_a, 0)

    def from_core_b(n, _):
        d = n * 2 + 1 - core
        remote(bnear(d), bnear(d), b_csend.at[n], b_crecv.at[n], sib).wait_recv()
        remote(bfar(d), bfar(d), f_csend.at[n], f_crecv.at[n], sib).wait_recv()
        return 0

    lax.fori_loop(0, nb * NX, from_core_b, 0)
    for cp in lists + local[:1] + local[3:]:
        cp.wait()

    def left(p, o):
        total = None
        for k in range(0, 16, 2):
            am = jnp.concatenate([a_all[amp_s[k + s, lax.rem(mine, 128) + 2 * p + o]] for s in (0, 1)], axis=1)
            bm = jnp.concatenate([b_all[cols_s[p, o, k + s]] for s in (0, 1)], axis=1)
            term = lax.dot_general(am, bm, NT, preferred_element_type=jnp.float32)
            total = term if total is None else total + term
        return total.astype(jnp.bfloat16)

    def partial(p):
        both = [left(p, o) for o in (0, 1)]
        return [lax.dot_general(both[o], b_all[tgts_s[p, 0, o]], NN, preferred_element_type=jnp.float32) for o in (0, 1)]

    def rcopy(i, o):
        n = (i - 1) * 2 + o
        return remote(part_s.at[n], part_r.at[n], r_send.at[n], r_recv.at[n], ldev(i))

    upper = pos // 2

    def one_dest(n, _):
        last = n // 3
        third = n // 2 - last
        second = lax.rem(n, 2) - last
        dest = ((1 - second - third - last) * 3 * (1 - upper) + second * (2 - upper)
                + third * (pos + 1 - 2 * lax.rem(pos, 2)) + last * pos)
        i = lax.rem(dest - pos + LINE, LINE)
        both = partial(dest)

        @pl.when(n < LINE - 1)
        def _():
            for o, r in enumerate(both):
                part_s[2 * i - 2 + o] = r.astype(jnp.bfloat16)
                rcopy(i, o).start()

        @pl.when(n == LINE - 1)
        def _():
            for o, r in enumerate(both):
                own[o] = r

        return 0

    lax.fori_loop(0, LINE, one_dest, 0)

    for i in (1, 2, 3):
        for cp in lcopies(i):
            cp.wait_send()
        for h in (0, 1):
            asend(h, 0, i, xdev(i)).wait_send()
            asend(h, 1, i, ydev(i)).wait_send()
        for j in (1, 2, 3):
            afwd(0, j, i, at(xp(j), y, core), ydev(i)).wait_send()
            afwd(1, j, i, at(x, yp(j), core), xdev(i)).wait_send()

    def core_sent(n, _):
        acore(n * 2 + core).wait_send()
        return 0

    lax.fori_loop(0, NX * NY, core_sent, 0)

    def bcore_sent(n, _):
        bcore(n * 2 + core).wait_send()
        fcore(n * 2 + core).wait_send()
        return 0

    lax.fori_loop(0, nb * NX, bcore_sent, 0)

    @pl.when(y < nb)
    def _():
        for i, j in others:
            fsend(i, j).wait_send()
        for i in (1, 2, 3):
            zcopy(i).wait_send()
            for h in (0, 1):
                bsend(h, 0, i, xdev(i)).wait_send()
                bsend(h, 1, i, ydev(i)).wait_send()
            for j in (1, 2, 3):
                bfwd(0, j, i, at(xp(j), y, core), ydev(i)).wait_send()

    for j in (1, 2, 3):
        @pl.when(yp(j) < nb)
        def _():
            for i in (1, 2, 3):
                bfwd(1, j, i, at(x, yp(j), core), xdev(i)).wait_send()

    for i in (1, 2, 3):
        for o in (0, 1):
            rcopy(i, o).wait_recv()
    for o in range(2):
        out_ref[o] = (own[o] + part_r[o].astype(jnp.float32) + part_r[2 + o].astype(jnp.float32)
                      + part_r[4 + o].astype(jnp.float32)).astype(jnp.bfloat16)
    for i in (1, 2, 3):
        for o in (0, 1):
            rcopy(i, o).wait_send()


def body(amplitudes, df_factors, out_tiles, pair_col, pair_amp):
    ts = amplitudes.shape[1]
    rows, cols = df_factors.shape
    ctiles = cols // ts
    pairs = pair_col.shape[1]
    dma = pltpu.SemaphoreType.DMA
    reg = pltpu.SemaphoreType.REGULAR
    chips = NX * NY
    anyw = pl.BlockSpec(memory_space=pl.ANY)
    return pl.pallas_call(
        kernel,
        out_shape=jax.ShapeDtypeStruct((2, ts, ts), jnp.bfloat16),
        in_specs=[anyw] * 5,
        out_specs=pl.BlockSpec(memory_space=pltpu.VMEM),
        scratch_shapes=[
            pltpu.VMEM((4 * 2 * chips, ts, ts), jnp.bfloat16),
            pltpu.VMEM((ctiles, QUAD * rows, ts), jnp.bfloat16),
            pltpu.VMEM((LINE, 2, pairs), jnp.int32),
            pltpu.VMEM((LINE, 1, 2), jnp.int32),
            pltpu.SMEM((pairs, 128), jnp.int32),
            pltpu.SMEM((LINE, 2, pairs), jnp.int32),
            pltpu.SMEM((LINE, 1, 2), jnp.int32),
            pltpu.VMEM((2, ts, ts), jnp.float32),
            pltpu.VMEM((6, ts, ts), jnp.bfloat16),
            pltpu.VMEM((6, ts, ts), jnp.bfloat16),
            dma((6 + ctiles,)), reg, reg((4,)), reg((4,)), dma((4,)), dma((4,)), dma((2, 4)), dma((2, 4)),
            dma((2, 2, 4)), dma((2, 4, 4)), dma((chips,)), dma((2, chips)), dma((chips,)),
            dma((2, 2, 4)), dma((2, 4, 4)), dma((chips,)), dma((2, chips)), dma((chips,)),
            dma((chips,)), dma((chips,)), dma((chips,)), dma((chips,)),
            dma((6,)), dma((6,)),
        ],
        compiler_params=pltpu.CompilerParams(
            collective_id=0, has_side_effects=True, vmem_limit_bytes=861 * 2**16),
        name="residual",
    )(pair_amp.T, pair_col, out_tiles[None], amplitudes, df_factors)


def solution(mesh):
    in_specs = (
        P("tile", None, None),
        P("aux", None),
        P(("tile", "aux")),
        P(("tile", "aux"), None),
        P(),
    )
    out_specs = P(("tile", "aux"), None, None)
    return jax.shard_map(body, mesh=mesh, in_specs=in_specs, out_specs=out_specs, check_vma=False)
```
